512 devices in a mesh: tile: 64 (over z, x_lo, core), tensor: 8 (over x_hi, y).
Axes of the slice: x: 4 (x_hi: 2, x_lo: 2; x = x_hi * 2 + x_lo), y: 4, z: 16, core: 2. Of those that a mesh axis runs over, the one named last changes fastest.
Arguments:
- tokens: bfloat16 [16384, 4096], P('tile'), may hold values from -6 to 6
- w_qkv: bfloat16 [3, 4096, 2048], P(None, 'tile', 'tensor'), may hold values from -0.09375 to 0.09375
- w_out: bfloat16 [2048, 4096], P('tensor', 'tile'), may hold values from -0.25 to 0.25
- window_ext: int32 [16, 3], P('tensor'), may hold values from 0 to 8, as said below
Outputs:
- mixed: bfloat16 [16384, 4096], P('tile', 'tensor')
The draws below stay inside these ranges and needn't reach their ends.
Inputs may be any that keep to these rules, and one draw needn't show every extreme that they name: `window_ext`: column 0 is at most 2, columns 1 and 2 lie from 1 to 4 and 1 to 8; each column's largest allowed value is taken by some head.
All inputs are finite; a program needn't handle non-finite values.
Results may differ from the reference program's by a relative error of at most 0.017.
Values may be sent and summed in bfloat16 or wider, within the bound.
A program may use at most 64 MiB of HBM per device.

```python
import jax
import jax.numpy as jnp
from jax import lax

D = 4096
HEADS = 16
HD = 128
TT = 2
TH = 8
TW = 16
GH = 4
GW = 4
RT = 2
RH = 4
RW = 8
TOK_DEV = 256
GT = 4
TOKENS = 16384
N_TILE = 64


def draw_window_ext(key, part):
    key = jax.random.fold_in(key, 11)
    keys = jax.random.split(key, 4)
    back = jax.random.randint(keys[0], (HEADS,), 0, TT + 1)
    rows = jax.random.randint(keys[1], (HEADS,), 1, TH // 2 + 1)
    cols = jax.random.randint(keys[2], (HEADS,), 1, TW // 2 + 1)
    chosen = jax.random.randint(keys[3], (3,), 0, HEADS)
    heads = jnp.arange(HEADS)
    back = jnp.where(heads == chosen[0], TT, back)
    rows = jnp.where(heads == chosen[1], TH // 2, rows)
    cols = jnp.where(heads == chosen[2], TW // 2, cols)
    return jnp.stack([back, rows, cols], axis=1).astype(jnp.int32)


def level_of(stream_key, extent, cuts, low, high):
    factor_of, own = 1.0, jax.random.fold_in(stream_key, 6)
    for position, blocks in cuts:
        steps = jnp.exp(jax.random.uniform(jax.random.fold_in(own, position), (blocks,), jnp.float32, low / len(cuts), high / len(cuts)))
        factor_of = factor_of * jnp.repeat(steps, extent[position] // blocks).reshape([-1 if axis == position else 1 for axis in range(len(extent))])
    return factor_of


def bell_draw(key, extent, scale, limit, cuts=(), held_as=jnp.bfloat16):
    result = scale * jax.random.normal(key, extent, jnp.float32)
    if cuts:
        result = result * level_of(key, extent, cuts, -0.22, 0.18)
    return jnp.clip(result, -limit, limit).astype(held_as)


def setup_inputs(seed: int = 0) -> dict:
    streams_of = jax.random.split(jax.random.key(seed), 5)
    tokens = bell_draw(streams_of[0], (TOKENS, D), 1.0, 6.0, ((0, 64),))
    w_qkv = bell_draw(streams_of[1], (3, D, HEADS * HD), D ** -0.5, 0.09375, ((1, 64), (2, 8)))
    w_out = bell_draw(streams_of[2], (HEADS * HD, D), (HEADS * HD // 4) ** -0.5, 0.25, ((0, 8), (1, 64)))
    window_ext = draw_window_ext(jax.random.fold_in(streams_of[4], 71), 0)
    return dict(tokens=tokens, w_qkv=w_qkv, w_out=w_out, window_ext=window_ext)


def unit_rows(proj):
    heads = proj.reshape(proj.shape[0], HEADS, HD)
    scale = lax.rsqrt(lax.optimization_barrier(jnp.mean(heads * heads, axis=-1, keepdims=True)) + 1e-06)
    return (heads * scale).astype(jnp.bfloat16)

def to_grid(values):
    grid = values.reshape(GT, GH, GW, TT, TH, TW, HEADS, HD)
    grid = jnp.transpose(grid, (0, 3, 1, 4, 2, 5, 6, 7))
    return grid.reshape(GT * TT, GH * TH, GW * TW, HEADS, HD)

def reference(tokens, w_qkv, w_out, window_ext):
    query = unit_rows(jnp.dot(tokens, w_qkv[0], preferred_element_type=jnp.float32))
    key = unit_rows(jnp.dot(tokens, w_qkv[1], preferred_element_type=jnp.float32))
    value = jnp.dot(tokens, w_qkv[2], preferred_element_type=jnp.float32).astype(jnp.bfloat16).reshape(TOKENS, HEADS, HD)
    frames = GT * TT
    rows = GH * TH
    cols = GW * TW
    pad = ((RT, 0), (RH, RH), (RW, RW), (0, 0), (0, 0))
    key_pad = jnp.pad(to_grid(key), pad)
    value_pad = jnp.pad(to_grid(value), pad)
    query_tiles = query.reshape(N_TILE, TOK_DEV, HEADS, HD)
    qa = jnp.arange(TT, dtype=jnp.int32)[:, None, None] + jnp.zeros((TT, TH, TW), jnp.int32)
    qb = jnp.arange(TH, dtype=jnp.int32)[None, :, None] + jnp.zeros((TT, TH, TW), jnp.int32)
    qc = jnp.arange(TW, dtype=jnp.int32)[None, None, :] + jnp.zeros((TT, TH, TW), jnp.int32)
    kshape = (TT + RT, TH + 2 * RH, TW + 2 * RW)
    ka = jnp.arange(kshape[0], dtype=jnp.int32)[:, None, None] + jnp.zeros(kshape, jnp.int32)
    kb = jnp.arange(kshape[1], dtype=jnp.int32)[None, :, None] + jnp.zeros(kshape, jnp.int32)
    kc = jnp.arange(kshape[2], dtype=jnp.int32)[None, None, :] + jnp.zeros(kshape, jnp.int32)
    nk = kshape[0] * kshape[1] * kshape[2]

    def one_tile(index):
        tile_t = index // (GH * GW)
        tile_h = index // GW % GH
        tile_w = index % GW
        start = (tile_t * TT, tile_h * TH, tile_w * TW, jnp.int32(0), jnp.int32(0))
        sizes = (kshape[0], kshape[1], kshape[2], HEADS, HD)
        keys = lax.dynamic_slice(key_pad, start, sizes).reshape(nk, HEADS, HD)
        vals = lax.dynamic_slice(value_pad, start, sizes).reshape(nk, HEADS, HD)
        q_f = (tile_t * TT + qa).reshape(-1)
        q_r = (tile_h * TH + qb).reshape(-1)
        q_c = (tile_w * TW + qc).reshape(-1)
        k_f = (tile_t * TT - RT + ka).reshape(-1)
        k_r = (tile_h * TH - RH + kb).reshape(-1)
        k_c = (tile_w * TW - RW + kc).reshape(-1)
        inside = (k_f >= 0) & (k_r >= 0) & (k_r < rows) & (k_c >= 0) & (k_c < cols)
        d_f = q_f[:, None] - k_f[None, :]
        d_r = jnp.abs(q_r[:, None] - k_r[None, :])
        d_c = jnp.abs(q_c[:, None] - k_c[None, :])
        seen = (d_f[None] >= 0) & (d_f[None] <= window_ext[:, 0, None, None])
        seen = seen & (d_r[None] <= window_ext[:, 1, None, None]) & (d_c[None] <= window_ext[:, 2, None, None])
        seen = seen & inside[None, None, :]
        scores = jnp.einsum('qhd,khd->hqk', query_tiles[index].astype(jnp.float32), keys.astype(jnp.float32)) / jnp.sqrt(jnp.float32(HD))
        weight = jnp.where(seen, jnp.exp(scores), jnp.float32(0.0))
        total = lax.optimization_barrier(jnp.sum(weight, axis=-1))
        weight_b = weight.astype(jnp.bfloat16)
        summed = jnp.einsum('hqk,khd->qhd', weight_b.astype(jnp.float32), vals.astype(jnp.float32))
        return (summed / jnp.transpose(total)[:, :, None]).astype(jnp.bfloat16)
    attended = lax.map(one_tile, jnp.arange(N_TILE, dtype=jnp.int32))
    attended = attended.reshape(TOKENS, HEADS * HD)
    return jnp.dot(attended, w_out, preferred_element_type=jnp.float32).astype(jnp.bfloat16)
```

```python
import functools

import jax
import jax.numpy as jnp
from jax import lax
from jax.experimental import pallas as pl
from jax.experimental.pallas import tpu as pltpu
from jax.sharding import PartitionSpec as P

MESH = pl.DeviceIdType.MESH
F32 = jnp.float32
BF16 = jnp.bfloat16
NZ = 16
SCALE = 128.0 ** -0.5


def kernel(win, tok_in, w_in, wo_in, out, tok, w, acc, kv, qs, mask, os, ts, attf, att, pk, wo,
           s_tok, s_init, s_bp, s_bm, s_ap, s_am, s_x, s_t, s_h, s_xe, s_wa, s_wc, s_ac, s_ax, s_ay):
    ti = lax.axis_index("tile")
    te = lax.axis_index("tensor")
    z, xl, c = ti // 4, (ti // 2) % 2, ti % 2
    xh, y = te // 4, te % 4
    t, h = z // 4, z % 4

    def at(z_, xl_, c_, xh_, y_):
        return (z_ * 4 + xl_ * 2 + c_, xh_ * 4 + y_)

    mate = at(z, xl, 1 - c, xh, y)
    side = at(z, 1 - xl, c, xh, y)
    side_mate = at(z, 1 - xl, 1 - c, xh, y)
    z_next = at((z + 1) % NZ, xl, c, xh, y)
    z_prev = at((z + NZ - 1) % NZ, xl, c, xh, y)
    later = at((z + 4) % NZ, xl, c, xh, y)
    earlier = at((z + NZ - 4) % NZ, xl, c, xh, y)

    def rc(src, dst, sems, i, dev):
        return pltpu.make_async_remote_copy(
            src_ref=src, dst_ref=dst, send_sem=sems.at[0, i], recv_sem=sems.at[1, i],
            device_id=dev, device_id_type=MESH)

    own_tok = pltpu.make_async_copy(tok_in, tok.at[c], s_tok.at[0, 1])
    own_tok.start()
    kv[...] = jnp.zeros_like(kv)

    bar = pltpu.get_barrier_semaphore()

    def greet(dev):
        pl.semaphore_signal(bar, inc=1, device_id=dev, device_id_type=MESH)

    for dev in (mate, side_mate, z_next, z_prev, later, earlier):
        greet(dev)
    for dx in range(4):
        for dy in range(4):
            if dx or dy:
                greet(at(z, xl ^ (dx & 1), c, xh ^ (dx >> 1), (y + dy) % 4))

    rows = pl.ds(pl.multiple_of(xl * 128, 128), 128)
    r0 = pl.ds(pl.multiple_of(xl * 128 + c * 64, 64), 64)
    mine = pl.ds(pl.multiple_of(c * 128, 128), 128)
    theirs = pl.ds(pl.multiple_of((1 - c) * 128, 128), 128)
    for j in range(3):
        w[z, j, r0, :] = w_in[j, :, mine]
    own_rows = wo_in[pl.ds(pl.multiple_of(c * 128, 128), 128), :]
    other_rows = wo_in[pl.ds(pl.multiple_of((1 - c) * 128, 128), 128), :]
    pk[0] = jnp.concatenate([other_rows, other_rows], axis=1)
    pl.semaphore_wait(bar, 21)

    i_mate = rc(w_in.at[:, :, theirs], w.at[z, pl.ds(0, 3), r0, :], s_init, 0, mate)
    i_side = rc(w_in.at[0, :, mine], w.at[z, 0, r0, :], s_init, 1, side)
    i_diag = rc(w_in.at[0, :, theirs], w.at[z, 0, r0, :], s_init, 2, side_mate)
    i_out = rc(pk.at[0], pk.at[1], s_init, 3, mate)
    i_mate.start()
    i_out.start()
    i_side.start()
    i_diag.start()
    tok_x = rc(tok_in, tok.at[c], s_tok, 0, mate)
    tok_x.start()

    i_mate.wait_recv()
    i_out.wait_recv()
    from_mate = pk[1]
    lane = lax.broadcasted_iota(jnp.int32, (128, 128), 1)
    own2 = jnp.concatenate([own_rows, own_rows], axis=1).astype(F32)
    keep = jnp.where(c == 0, lane, 127 - lane) < 64
    w[z, 3, rows, :] = jnp.where(keep, own2, from_mate.astype(F32)).astype(BF16)

    def part_b(zo):
        return w.at[zo, pl.ds(1, 3), rows, :]

    def part_a(zo):
        return w.at[zo, 0]

    def part_x(zo):
        return w.at[zo, pl.ds(1, 2), rows, :]

    def send_b(zo, sems, i, dev):
        return rc(part_b(zo), part_b(zo), sems, i, dev)

    def send_a(zo, sems, i, dev):
        return rc(part_a(zo), part_a(zo), sems, i, dev)

    def send_x(zo, i):
        return rc(part_x(zo), part_x(zo), s_x, i, side)

    send_b(z, s_bp, 0, z_next).start()
    send_b(z, s_bm, 0, z_prev).start()
    send_x(z, 0).start()
    i_side.wait_recv()
    i_diag.wait_recv()
    send_a(z, s_ap, 0, z_next).start()
    send_a(z, s_am, 0, z_prev).start()

    rh, rw, rt = win[c, 1], win[c, 2], win[c, 0]
    qi = lax.broadcasted_iota(jnp.int32, (64, 384), 0)
    ki = lax.broadcasted_iota(jnp.int32, (64, 384), 1)
    grp = ki // 128
    krow = (ki % 128) // 8
    d_r = jnp.abs(krow - 4 - qi // 8)
    d_c = jnp.abs((grp - 1) * 8 + ki % 8 - qi % 8)
    grow = h * 8 + krow - 4
    near = (d_r <= rh) & (d_c <= rw) & (grow >= 0) & (grow < 32)
    for u in range(4):
        gcol = xl * 4 + u + grp - 1
        mask[u] = jnp.where(near & (gcol >= 0) & (gcol < 8), F32(1.0), F32(0.0))

    def allow(a, f):
        df = 2 + a - f
        ok = jnp.where(rt >= df, F32(1.0), F32(0.0))
        if f < 2:
            ok = jnp.where(t > 0, ok, F32(0.0))
        return ok

    own_tok.wait()
    tok_x.wait_recv()

    def project(zo):
        cols = pl.ds(pl.multiple_of(zo * 256, 256), 256)
        lhs = tok[:, :, cols].reshape(512, 256)
        rhs = jnp.concatenate([w[zo, 0], w[zo, 1], w[zo, 2]], axis=1)
        return jnp.dot(lhs, rhs, preferred_element_type=F32)

    send_x(z, 0).wait_recv()
    acc[...] = project(z)

    def fwd(s, _):
        zp = (z + NZ - s) % NZ
        zm = (z + s) % NZ

        @pl.when(s < 8)
        def _():
            send_b(zp, s_bp, s - 1, z_next).wait_recv()

            @pl.when(s < 7)
            def _():
                send_b(zp, s_bp, s, z_next).start()
            send_x(zp, s).start()

        send_b(zm, s_bm, s - 1, z_prev).wait_recv()

        @pl.when(s < 8)
        def _():
            send_b(zm, s_bm, s, z_prev).start()
        send_x(zm, 7 + s).start()

        send_a(zp, s_ap, s - 1, z_next).wait_recv()

        @pl.when(s < 8)
        def _():
            send_a(zp, s_ap, s, z_next).start()
            send_a(zm, s_am, s - 1, z_prev).wait_recv()

            @pl.when(s < 7)
            def _():
                send_a(zm, s_am, s, z_prev).start()

        @pl.when(s > 1)
        def _():
            zq = (z + NZ - s + 1) % NZ
            send_x(zq, s - 1).wait_recv()
            acc[...] += project(zq)
            zr = (z + s - 1) % NZ
            send_x(zr, 6 + s).wait_recv()
            acc[...] += project(zr)
        return 0

    lax.fori_loop(1, 9, fwd, 0)
    z8 = (z + 8) % NZ
    send_x(z8, 15).wait_recv()
    acc[...] += project(z8)

    def unit(p):
        return p * lax.rsqrt(jnp.mean(p * p, axis=-1, keepdims=True) + 1e-06)

    for tw in range(2):
        for a in range(2):
            at_rows = pl.ds(tw * 256 + a * 128, 128)
            both = jnp.concatenate([unit(acc[at_rows, 128:256]), acc[at_rows, 256:384]], axis=1)
            both = both.reshape(8, 2, 8, 256)
            for g in range(2):
                kv[2 + a, 1 + tw * 2 + g, 32:96, :] = both[:, g].reshape(64, 256).astype(BF16)

    edge_out = 4 - 3 * xl
    edge_in = 5 * xl
    OWN, TOP, BOT = pl.ds(32, 64), pl.ds(0, 32), pl.ds(96, 32)
    MIDG = pl.ds(1, 4)

    def t_halo(f):
        return rc(kv.at[2 + f, MIDG, OWN, :], kv.at[f, MIDG, OWN, :], s_t, f, later)

    def h_down(p):
        fr = pl.ds(2 * p, 2)
        return rc(kv.at[fr, MIDG, pl.ds(64, 32), :], kv.at[fr, MIDG, TOP, :], s_h, p, z_next)

    def h_up(p):
        fr = pl.ds(2 * p, 2)
        return rc(kv.at[fr, MIDG, pl.ds(32, 32), :], kv.at[fr, MIDG, BOT, :], s_h, 2 + p, z_prev)

    def x_edge(p, part):
        fr = pl.ds(2 * p, 2)
        rws = (OWN, TOP, BOT)[part]
        return rc(kv.at[fr, edge_out, rws, :], kv.at[fr, edge_in, rws, :], s_xe, p * 3 + part, side)

    has_prev, has_later = t > 0, t < 3
    has_up, has_down = h > 0, h < 3

    @pl.when(has_down)
    def _():
        h_down(1).start()

    @pl.when(has_up)
    def _():
        h_up(1).start()

    @pl.when(has_later)
    def _():
        t_halo(1).start()
        t_halo(0).start()

    x_edge(1, 0).start()

    def wa(dx, dy):
        xh2, y2 = xh ^ (dx >> 1), (y + dy) % 4
        j2 = xh2 * 4 + y2
        src = w.at[pl.ds(2 * j2, 2), 3, rows, :]
        return rc(src, wo.at[c, xh * 4 + y, xl], s_wa, dx * 4 + dy, at(z, xl ^ (dx & 1), c, xh2, y2))

    for dx in range(4):
        for dy in range(4):
            if dx or dy:
                wa(dx, dy).start()
    own_wo = pltpu.make_async_copy(w.at[pl.ds(2 * te, 2), 3, rows, :], wo.at[c, te, xl], s_wa.at[0, 0])
    own_wo.start()

    for tw in range(2):
        for a in range(2):
            q = unit(acc[pl.ds(tw * 256 + a * 128, 128), 0:128]).reshape(8, 2, 8, 128)
            for g in range(2):
                qs[tw * 2 + g, a] = q[:, g].reshape(64, 128).astype(BF16)

    @pl.when(has_up)
    def _():
        h_down(1).wait_recv()
        x_edge(1, 1).start()

    @pl.when(has_down)
    def _():
        h_up(1).wait_recv()
        x_edge(1, 2).start()

    x_edge(1, 0).wait_recv()

    @pl.when(has_up)
    def _():
        x_edge(1, 1).wait_recv()

    @pl.when(has_down)
    def _():
        x_edge(1, 2).wait_recv()

    def attend(u, a, f):
        keys = kv[f, u:u + 3, :, 0:128].reshape(384, 128)
        vals = kv[f, u:u + 3, :, 128:256].reshape(384, 128)
        s = lax.dot_general(qs[u, a], keys, (((1,), (1,)), ((), ())), preferred_element_type=F32)
        wt = jnp.exp(s * SCALE) * (mask[u] * allow(a, f))
        part = wt[:, 0:128] + wt[:, 128:256] + wt[:, 256:384]
        return jnp.dot(wt.astype(BF16), vals, preferred_element_type=F32), part

    for u in range(4):
        o, p = attend(u, 0, 2)
        os[u, 0] = o
        ts[u, 0] = p
        o2, p2 = attend(u, 1, 2)
        o3, p3 = attend(u, 1, 3)
        os[u, 1] = o2 + o3
        ts[u, 1] = p2 + p3

    @pl.when(has_prev)
    def _():
        t_halo(1).wait_recv()
        t_halo(0).wait_recv()

        @pl.when(has_down)
        def _():
            h_down(0).start()

        @pl.when(has_up)
        def _():
            h_up(0).start()
        x_edge(0, 0).start()

        @pl.when(has_up)
        def _():
            h_down(0).wait_recv()
            x_edge(0, 1).start()

        @pl.when(has_down)
        def _():
            h_up(0).wait_recv()
            x_edge(0, 2).start()
        x_edge(0, 0).wait_recv()

        @pl.when(has_up)
        def _():
            x_edge(0, 1).wait_recv()

        @pl.when(has_down)
        def _():
            x_edge(0, 2).wait_recv()

    for u in range(4):
        for a in range(2):
            o, p = attend(u, a, 1)
            if a == 0:
                o2, p2 = attend(u, 0, 0)
                o, p = o + o2, p + p2
            total = jnp.sum(ts[u, a] + p, axis=-1, keepdims=True)
            res = (os[u, a] + o) / total
            attf[u // 2, a, :, u % 2] = res.reshape(8, 8, 128)

    for tw in range(2):
        pk2 = attf[tw].reshape(256, 128).astype(BF16)
        ts_dst = att.at[8 + tw]
        ts_dst[0] = pk2

    a_mate = rc(att.at[9 - c, 0], att.at[te, c], s_ac, 0, mate)
    a_mate.start()
    att[te, c] = att[8 + c, 0]
    a_mate.wait_recv()

    def a_side(j, i, dev):
        return rc(att.at[j], att.at[j], s_ay, i, dev)

    te_x = (1 - xh) * 4 + y
    ax = rc(att.at[te], att.at[te], s_ax, 0, at(z, xl, c, 1 - xh, y))
    ax.start()
    for dy in (1, 3, 2):
        a_side(te, dy, at(z, xl, c, xh, (y + dy) % 4)).start()

    own_wo.wait()
    for dx in range(4):
        for dy in range(4):
            if dx or dy:
                rc(w.at[pl.ds(0, 2), 3, rows, :], wo.at[c, 0, 0], s_wa, dx * 4 + dy, mate).wait_recv()
    wo_x = rc(wo.at[c], wo.at[c], s_wc, 0, mate)
    wo_x.start()

    ax.wait_recv()
    for dy in (1, 3, 2):
        a_side(te_x, 4 + dy, at(z, xl, c, xh, (y + dy) % 4)).start()
    wo_x.wait_recv()

    def term(j):
        lhs = jnp.concatenate([att[j, 0], att[j, 1]], axis=1)
        rhs = jnp.concatenate([
            jnp.concatenate([wo[p, j, 0, 0], wo[p, j, 1, 0], wo[p, j, 0, 1], wo[p, j, 1, 1]], axis=1)
            for p in range(2)], axis=0)
        return jnp.dot(lhs, rhs, preferred_element_type=F32)

    fin = acc.at[pl.ds(0, 256), :]
    fin2 = acc.at[pl.ds(256, 256), :]

    def add(j, first=False):
        r = term(j)
        if first:
            fin[...] = r[:, 0:384]
            fin2[:, 0:128] = r[:, 384:512]
        else:
            fin[...] += r[:, 0:384]
            fin2[:, 0:128] += r[:, 384:512]

    add(te, True)
    add(te_x)
    for k in range(2):
        for dy in (1, 3, 2):
            a_side(te, 4 * k + dy, mate).wait_recv()
            xs = xh if k == 0 else 1 - xh
            add(xs * 4 + (y + 4 - dy) % 4)
    out[:, 0:384] = fin[...].astype(BF16)
    out[:, 384:512] = fin2[:, 0:128].astype(BF16)

    for d in (i_mate, i_side, i_diag, i_out, tok_x, a_mate, ax, wo_x):
        d.wait_send()

    def drain(s, _):
        send_x(z, s).wait_send()

        @pl.when(s < 8)
        def _():
            send_b(z, s_bm, s, z_prev).wait_send()
            send_a(z, s_ap, s, z_next).wait_send()

        @pl.when(s < 7)
        def _():
            send_b(z, s_bp, s, z_next).wait_send()
            send_a(z, s_am, s, z_prev).wait_send()
        return 0

    lax.fori_loop(0, 16, drain, 0)
    for dx in range(4):
        for dy in range(4):
            if dx or dy:
                wa(dx, dy).wait_send()
    for k in range(2):
        for dy in (1, 3, 2):
            a_side(te, 4 * k + dy, mate).wait_send()
    x_edge(1, 0).wait_send()

    @pl.when(has_later)
    def _():
        t_halo(0).wait_send()
        t_halo(1).wait_send()

    @pl.when(has_prev)
    def _():
        x_edge(0, 0).wait_send()

    @pl.when(has_down)
    def _():
        h_down(1).wait_send()
        x_edge(1, 2).wait_send()

        @pl.when(has_prev)
        def _():
            h_down(0).wait_send()
            x_edge(0, 2).wait_send()

    @pl.when(has_up)
    def _():
        h_up(1).wait_send()
        x_edge(1, 1).wait_send()

        @pl.when(has_prev)
        def _():
            h_up(0).wait_send()
            x_edge(0, 1).wait_send()


def per_device(tokens, w_qkv, w_out, window_ext):
    vm = pl.BlockSpec(memory_space=pltpu.VMEM)
    dma = lambda n: pltpu.SemaphoreType.DMA((2, n))
    return pl.pallas_call(
        kernel,
        out_shape=jax.ShapeDtypeStruct((256, 512), BF16),
        in_specs=[pl.BlockSpec(memory_space=pltpu.SMEM), pl.BlockSpec(memory_space=pl.ANY), vm, vm],
        out_specs=vm,
        scratch_shapes=[
            pltpu.VMEM((2, 256, 4096), BF16),
            pltpu.VMEM((16, 4, 256, 128), BF16),
            pltpu.VMEM((512, 384), F32),
            pltpu.VMEM((4, 6, 128, 256), BF16),
            pltpu.VMEM((4, 2, 64, 128), BF16),
            pltpu.VMEM((4, 64, 384), F32),
            pltpu.VMEM((4, 2, 64, 128), F32),
            pltpu.VMEM((4, 2, 64, 128), F32),
            pltpu.VMEM((2, 2, 8, 2, 8, 128), F32),
            pltpu.VMEM((10, 2, 256, 128), BF16),
            pltpu.VMEM((2, 128, 128), BF16),
            pltpu.VMEM((2, 8, 2, 2, 128, 128), BF16),
            dma(2), dma(4), dma(8), dma(8), dma(8), dma(8), dma(16), dma(2), dma(4), dma(6),
            dma(16), dma(1), dma(1), dma(1), dma(8),
        ],
        compiler_params=pltpu.CompilerParams(
            collective_id=0, has_side_effects=True, vmem_limit_bytes=56 * 2 ** 20),
        name="tile_attention",
    )(window_ext, tokens, w_qkv, w_out)


def solution(mesh):
    in_specs = (P("tile", None), P(None, "tile", "tensor"), P("tensor", "tile"), P("tensor", None))
    return jax.shard_map(
        per_device, mesh=mesh, in_specs=in_specs, out_specs=P("tile", "tensor"), check_vma=False)
```

```python
import functools

import jax
import jax.numpy as jnp
from jax import lax
from jax.experimental import pallas as pl
from jax.experimental.pallas import tpu as pltpu
from jax.sharding import PartitionSpec as P

MESH = pl.DeviceIdType.MESH
F32 = jnp.float32
BF16 = jnp.bfloat16
NZ = 16
SCALE = 128.0 ** -0.5


def kernel(win, tok_in, w_in, wo_in, out, tok, w, acc, kv, qs, mask, os, ts, attf, att, tmp, wo, fin,
           s_tok, s_init, s_zp, s_zm, s_x, s_t, s_h, s_xe, s_wa, s_wc, s_ag):
    ti = lax.axis_index("tile")
    te = lax.axis_index("tensor")
    z, xl, c = ti // 4, (ti // 2) % 2, ti % 2
    xh, y = te // 4, te % 4
    t, h = z // 4, z % 4

    def at(z_, xl_, c_, xh_, y_):
        return (z_ * 4 + xl_ * 2 + c_, xh_ * 4 + y_)

    zn, zv = (z + 1) % NZ, (z + NZ - 1) % NZ
    mate = at(z, xl, 1 - c, xh, y)
    side = at(z, 1 - xl, c, xh, y)
    side_mate = at(z, 1 - xl, 1 - c, xh, y)
    z_next = at(zn, xl, c, xh, y)
    z_prev = at(zv, xl, c, xh, y)
    side_next = at(zn, 1 - xl, c, xh, y)
    side_prev = at(zv, 1 - xl, c, xh, y)
    later = at((z + 4) % NZ, xl, c, xh, y)
    earlier = at((z + NZ - 4) % NZ, xl, c, xh, y)

    def rc(src, dst, sems, i, dev):
        return pltpu.make_async_remote_copy(
            src_ref=src, dst_ref=dst, send_sem=sems.at[0, i], recv_sem=sems.at[1, i],
            device_id=dev, device_id_type=MESH)

    def rc2(src, dst, si, ri, sems, dev):
        return pltpu.make_async_remote_copy(
            src_ref=src, dst_ref=dst, send_sem=sems.at[0, si], recv_sem=sems.at[1, ri],
            device_id=dev, device_id_type=MESH)

    rows = pl.ds(pl.multiple_of(xl * 128, 128), 128)
    others = pl.ds(pl.multiple_of((1 - xl) * 128, 128), 128)
    r0 = pl.ds(pl.multiple_of(xl * 128 + c * 64, 64), 64)
    mine = pl.ds(pl.multiple_of(c * 128, 128), 128)
    theirs = pl.ds(pl.multiple_of((1 - c) * 128, 128), 128)

    own_w = pltpu.make_async_copy(w_in.at[:, :, mine], w.at[z, pl.ds(0, 3), r0, :], s_tok.at[0, 2])
    own_o = pltpu.make_async_copy(wo_in.at[:, mine], w.at[z, 3, r0, :], s_tok.at[0, 3])
    own_tok = pltpu.make_async_copy(tok_in, tok.at[c], s_tok.at[0, 1])
    for d in (own_w, own_o, own_tok):
        d.start()

    bar = pltpu.get_barrier_semaphore()

    def greet(dev):
        pl.semaphore_signal(bar, inc=1, device_id=dev, device_id_type=MESH)

    kv[...] = jnp.zeros_like(kv)
    for dev in (later, earlier, z_next, z_prev, side_next, side_prev, side_mate, mate):
        greet(dev)
    for dx in range(4):
        for dy in range(4):
            if dx or dy:
                greet(at(z, xl ^ (dx & 1), c, xh ^ (dx >> 1), (y + dy) % 4))
    for dx, dy in ((2, 0), (0, 1), (0, 2), (0, 3)):
        greet(at(z, xl, 1 - c, xh ^ (dx >> 1), (y + dy) % 4))
    pl.semaphore_wait(bar, 27)

    i_mate = rc(w_in.at[:, :, theirs], w.at[z, pl.ds(0, 3), r0, :], s_init, 0, mate)
    i_side = rc(w_in.at[0, :, mine], w.at[z, 0, r0, :], s_init, 1, side)
    i_diag = rc(w_in.at[0, :, theirs], w.at[z, 0, r0, :], s_init, 2, side_mate)
    i_out = rc(wo_in.at[:, theirs], w.at[z, 3, r0, :], s_init, 3, mate)
    i_mate.start()
    i_out.start()
    i_side.start()
    i_diag.start()
    tok_x = rc(tok_in, tok.at[c], s_tok, 0, mate)
    tok_x.start()

    def chunk(zo, ch):
        return w.at[zo, (1, 2, 0, 0, 3)[ch], others if ch == 3 else rows, :]

    def zp_copy(zo, ch, s):
        return rc(chunk(zo, ch), chunk(zo, ch), s_zp, ch * 8 + s, z_next)

    def zm_copy(zo, ch, s):
        return rc(chunk(zo, ch), chunk(zo, ch), s_zm, ch * 8 + s, z_prev)

    def x_copy(zo, m, i):
        return rc(chunk(zo, m), chunk(zo, m), s_x, m * 16 + i, side)

    own_w.wait()
    i_mate.wait_recv()
    for ch in range(2):
        zp_copy(z, ch, 0).start()
        zm_copy(z, ch, 0).start()
        x_copy(z, ch, 0).start()
    zp_copy(z, 2, 0).start()
    zm_copy(z, 2, 0).start()
    own_o.wait()
    i_out.wait_recv()
    i_side.wait_recv()
    i_diag.wait_recv()
    for ch in (3, 4):
        zp_copy(z, ch, 0).start()
        zm_copy(z, ch, 0).start()

    rh, rw, rt = win[c, 1], win[c, 2], win[c, 0]
    qi = lax.broadcasted_iota(jnp.int32, (64, 384), 0)
    ki = lax.broadcasted_iota(jnp.int32, (64, 384), 1)
    grp = ki // 128
    krow = (ki % 128) // 8
    d_r = jnp.abs(krow - 4 - qi // 8)
    d_c = jnp.abs((grp - 1) * 8 + ki % 8 - qi % 8)
    grow = h * 8 + krow - 4
    near = (d_r <= rh) & (d_c <= rw) & (grow >= 0) & (grow < 32)
    for u in range(4):
        gcol = xl * 4 + u + grp - 1
        mask[u] = jnp.where(near & (gcol >= 0) & (gcol < 8), F32(1.0), F32(0.0))

    def allow(a, f):
        df = 2 + a - f
        ok = jnp.where(rt >= df, F32(1.0), F32(0.0))
        if f < 2:
            ok = jnp.where(t > 0, ok, F32(0.0))
        return ok

    def project(zo):
        cols = pl.ds(pl.multiple_of(zo * 256, 256), 256)
        lhs = tok[:, :, cols].reshape(512, 256)
        rhs = jnp.concatenate([w[zo, 0], w[zo, 1], w[zo, 2]], axis=1)
        return jnp.dot(lhs, rhs, preferred_element_type=F32)

    def fwd(s, _):
        zp = (z + NZ - s) % NZ
        zm = (z + s) % NZ

        for ch in range(5):
            q_part = ch in (2, 3)
            last_p, last_m = (8, 7) if q_part else (7, 8)

            @pl.when(s <= last_p)
            def _():
                zp_copy(zp, ch, s - 1).wait_recv()

                @pl.when(s < last_p)
                def _():
                    zp_copy(zp, ch, s).start()
                if ch < 2:
                    x_copy(zp, ch, s).start()

            @pl.when(s <= last_m)
            def _():
                zm_copy(zm, ch, s - 1).wait_recv()

                @pl.when(s < last_m)
                def _():
                    zm_copy(zm, ch, s).start()
                if ch < 2:
                    x_copy(zm, ch, 7 + s).start()

        @pl.when(s == 1)
        def _():
            own_tok.wait()
            tok_x.wait_recv()
            x_copy(z, 0, 0).wait_recv()
            x_copy(z, 1, 0).wait_recv()
            acc[...] = project(z)

        @pl.when(s > 1)
        def _():
            zq = (z + NZ - s + 1) % NZ
            x_copy(zq, 0, s - 1).wait_recv()
            x_copy(zq, 1, s - 1).wait_recv()
            acc[...] += project(zq)
            zr = (z + s - 1) % NZ
            x_copy(zr, 0, 6 + s).wait_recv()
            x_copy(zr, 1, 6 + s).wait_recv()
            acc[...] += project(zr)
        return 0

    lax.fori_loop(1, 9, fwd, 0)
    z8 = (z + 8) % NZ
    x_copy(z8, 0, 15).wait_recv()
    x_copy(z8, 1, 15).wait_recv()
    acc[...] += project(z8)

    def unit(p):
        return p * lax.rsqrt(jnp.mean(p * p, axis=-1, keepdims=True) + 1e-06)

    for tw in range(2):
        for a in range(2):
            at_rows = pl.ds(tw * 256 + a * 128, 128)
            both = jnp.concatenate([unit(acc[at_rows, 128:256]), acc[at_rows, 256:384]], axis=1)
            both = both.reshape(8, 2, 8, 256)
            for g in range(2):
                kv[2 + a, 1 + tw * 2 + g, 32:96, :] = both[:, g].reshape(64, 256).astype(BF16)

    edge_out = 4 - 3 * xl
    edge_in = 5 * xl
    OWN, TOP, BOT = pl.ds(32, 64), pl.ds(0, 32), pl.ds(96, 32)
    UP, DOWN = pl.ds(32, 32), pl.ds(64, 32)
    MIDG = pl.ds(1, 4)
    FRAMES = (pl.ds(2, 2), pl.ds(1, 1), pl.ds(0, 1))

    def t_halo(f):
        return rc(kv.at[2 + f, MIDG, OWN, :], kv.at[f, MIDG, OWN, :], s_t, f, later)

    def h_down(i):
        return rc(kv.at[FRAMES[i], MIDG, DOWN, :], kv.at[FRAMES[i], MIDG, TOP, :], s_h, i, z_next)

    def h_up(i):
        return rc(kv.at[FRAMES[i], MIDG, UP, :], kv.at[FRAMES[i], MIDG, BOT, :], s_h, 3 + i, z_prev)

    def x_own(i):
        return rc(kv.at[FRAMES[i], edge_out, OWN, :], kv.at[FRAMES[i], edge_in, OWN, :], s_xe, i, side)

    def x_down(i):
        return rc(kv.at[FRAMES[i], edge_out, DOWN, :], kv.at[FRAMES[i], edge_in, TOP, :], s_xe, 3 + i, side_next)

    def x_up(i):
        return rc(kv.at[FRAMES[i], edge_out, UP, :], kv.at[FRAMES[i], edge_in, BOT, :], s_xe, 6 + i, side_prev)

    has_prev, has_later = t > 0, t < 3
    has_up, has_down = h > 0, h < 3

    def halo_start(i):
        @pl.when(has_down)
        def _():
            h_down(i).start()
            x_down(i).start()

        @pl.when(has_up)
        def _():
            h_up(i).start()
            x_up(i).start()
        x_own(i).start()

    def halo_wait(i):
        x_own(i).wait_recv()

        @pl.when(has_up)
        def _():
            h_down(i).wait_recv()
            x_down(i).wait_recv()

        @pl.when(has_down)
        def _():
            h_up(i).wait_recv()
            x_up(i).wait_recv()

    def halo_sent(i):
        x_own(i).wait_send()

        @pl.when(has_down)
        def _():
            h_down(i).wait_send()
            x_down(i).wait_send()

        @pl.when(has_up)
        def _():
            h_up(i).wait_send()
            x_up(i).wait_send()

    @pl.when(has_later)
    def _():
        t_halo(1).start()
    halo_start(0)

    def wa(dx, dy):
        xh2, y2 = xh ^ (dx >> 1), (y + dy) % 4
        j2 = xh2 * 4 + y2
        src = w.at[pl.ds(2 * j2, 2), 3, rows, :]
        return rc(src, wo.at[c, xh * 4 + y, xl], s_wa, dx * 4 + dy, at(z, xl ^ (dx & 1), c, xh2, y2))

    for dx in range(4):
        for dy in range(4):
            if dx or dy:
                wa(dx, dy).start()
    own_wo = pltpu.make_async_copy(w.at[pl.ds(2 * te, 2), 3, rows, :], wo.at[c, te, xl], s_wa.at[0, 0])
    own_wo.start()

    for tw in range(2):
        for a in range(2):
            q = unit(acc[pl.ds(tw * 256 + a * 128, 128), 0:128]).reshape(8, 2, 8, 128)
            for g in range(2):
                qs[tw * 2 + g, a] = q[:, g].reshape(64, 128).astype(BF16)

    def attend(u, a, f):
        keys = kv[f, u:u + 3, :, 0:128].reshape(384, 128)
        vals = kv[f, u:u + 3, :, 128:256].reshape(384, 128)
        s = lax.dot_general(qs[u, a], keys, (((1,), (1,)), ((), ())), preferred_element_type=F32)
        wt = jnp.exp(s * SCALE) * (mask[u] * allow(a, f))
        part = wt[:, 0:128] + wt[:, 128:256] + wt[:, 256:384]
        return jnp.dot(wt.astype(BF16), vals, preferred_element_type=F32), part

    halo_wait(0)
    for u in range(4):
        o, p = attend(u, 0, 2)
        os[u, 0] = o
        ts[u, 0] = p
        o2, p2 = attend(u, 1, 2)
        o3, p3 = attend(u, 1, 3)
        os[u, 1] = o2 + o3
        ts[u, 1] = p2 + p3

    @pl.when(has_later)
    def _():
        t_halo(1).wait_send()
        t_halo(0).start()

    te_x = (1 - xh) * 4 + y

    def slot(a, k, dy, p):
        return ((a * 2 + k) * 4 + dy) * 2 + p

    def a_out(a, k, dy, own):
        src = att.at[te, c, a] if own else tmp.at[1 - c, a]
        dev = at(z, xl, c if own else 1 - c, 1 - xh if k else xh, (y + dy) % 4)
        return rc2(src, att.at[te, c, a], slot(a, k, dy, 0 if own else 1), slot(a, k, dy, c), s_ag, dev)

    def a_on(a, dy, p):
        return rc(att.at[te_x, p, a], att.at[te_x, p, a], s_ag, slot(a, 1, dy, p), at(z, xl, c, xh, (y + dy) % 4))

    def a_in(a, k, dy, p):
        return rc(att.at[te, p, a], att.at[te, p, a], s_ag, slot(a, k, dy, p), mate)

    def finish(a, f):
        for u in range(4):
            o, p = attend(u, a, f)
            total = jnp.sum(ts[u, a] + p, axis=-1, keepdims=True)
            res = (os[u, a] + o) / total
            attf[u // 2, :, u % 2] = res.reshape(8, 8, 128)
        for tw in range(2):
            tmp[tw, a] = attf[tw].reshape(128, 128).astype(BF16)
        att[te, c, a] = tmp[c, a]
        a_out(a, 1, 0, True).start()
        a_out(a, 1, 0, False).start()
        a_out(a, 0, 0, False).start()
        for dy in (1, 3, 2):
            a_out(a, 0, dy, True).start()
            a_out(a, 0, dy, False).start()

    def spread_on(a):
        for p in range(2):
            a_in(a, 1, 0, p).wait_recv()
            for dy in (1, 3, 2):
                a_on(a, dy, p).start()

    def term(j, a):
        lhs = jnp.concatenate([att[j, 0, a], att[j, 1, a]], axis=1)
        rhs = jnp.concatenate([
            jnp.concatenate([wo[0, j, x, k], wo[1, j, x, k]], axis=1)
            for k in range(2) for x in range(2)], axis=0)
        return lax.dot_general(lhs, rhs, (((1,), (1,)), ((), ())), preferred_element_type=F32)

    def mix(a):
        tot = fin.at[a]
        rc2(att.at[te, 0, a], att.at[te, 0, a], 0, slot(a, 0, 0, 1 - c), s_ag, mate).wait_recv()
        tot[...] = term(te, a)
        tot[...] += term(te_x, a)
        for k in range(2):
            for dy in (1, 3, 2):
                a_in(a, k, dy, 0).wait_recv()
                a_in(a, k, dy, 1).wait_recv()
                xs = xh if k == 0 else 1 - xh
                tot[...] += term(xs * 4 + (y + 4 - dy) % 4, a)
        out[a * 128:(a + 1) * 128, :] = tot[...].astype(BF16)

    @pl.when(has_prev)
    def _():
        t_halo(1).wait_recv()
        halo_start(1)

    own_wo.wait()
    for dx in range(4):
        for dy in range(4):
            if dx or dy:
                wa(dx, dy).wait_recv()
    wo_x = rc(wo.at[c], wo.at[c], s_wc, 0, mate)
    wo_x.start()

    @pl.when(has_prev)
    def _():
        halo_wait(1)
    finish(1, 1)

    for u in range(4):
        o, p = attend(u, 0, 1)
        os[u, 0] += o
        ts[u, 0] += p
    @pl.when(has_prev)
    def _():
        t_halo(0).wait_recv()
        halo_start(2)
    spread_on(1)

    @pl.when(has_prev)
    def _():
        halo_wait(2)
    finish(0, 0)
    spread_on(0)
    wo_x.wait_recv()
    mix(1)
    mix(0)

    for d in (i_mate, i_side, i_diag, i_out, tok_x, wo_x):
        d.wait_send()

    def drain(s, _):
        for m in range(2):
            x_copy(z, m, s).wait_send()

        @pl.when(s < 8)
        def _():
            for ch in range(5):
                (zp_copy if ch in (2, 3) else zm_copy)(z, ch, s).wait_send()

        @pl.when(s < 7)
        def _():
            for ch in range(5):
                (zm_copy if ch in (2, 3) else zp_copy)(z, ch, s).wait_send()
        return 0

    lax.fori_loop(0, 16, drain, 0)
    for dx in range(4):
        for dy in range(4):
            if dx or dy:
                wa(dx, dy).wait_send()
    for a in range(2):
        a_out(a, 1, 0, True).wait_send()
        a_out(a, 1, 0, False).wait_send()
        a_out(a, 0, 0, False).wait_send()
        for dy in (1, 3, 2):
            a_out(a, 0, dy, True).wait_send()
            a_out(a, 0, dy, False).wait_send()
            a_on(a, dy, 0).wait_send()
            a_on(a, dy, 1).wait_send()
    halo_sent(0)

    @pl.when(has_later)
    def _():
        t_halo(0).wait_send()

    @pl.when(has_prev)
    def _():
        halo_sent(1)
        halo_sent(2)


def per_device(tokens, w_qkv, w_out, window_ext):
    vm = pl.BlockSpec(memory_space=pltpu.VMEM)
    hbm = pl.BlockSpec(memory_space=pl.ANY)
    dma = lambda n: pltpu.SemaphoreType.DMA((2, n))
    return pl.pallas_call(
        kernel,
        out_shape=jax.ShapeDtypeStruct((256, 512), BF16),
        in_specs=[pl.BlockSpec(memory_space=pltpu.SMEM), hbm, hbm, hbm],
        out_specs=vm,
        scratch_shapes=[
            pltpu.VMEM((2, 256, 4096), BF16),
            pltpu.VMEM((16, 4, 256, 128), BF16),
            pltpu.VMEM((512, 384), F32),
            pltpu.VMEM((4, 6, 128, 256), BF16),
            pltpu.VMEM((4, 2, 64, 128), BF16),
            pltpu.VMEM((4, 64, 384), F32),
            pltpu.VMEM((4, 2, 64, 128), F32),
            pltpu.VMEM((4, 2, 64, 128), F32),
            pltpu.VMEM((2, 8, 2, 8, 128), F32),
            pltpu.VMEM((8, 2, 2, 128, 128), BF16),
            pltpu.VMEM((2, 2, 128, 128), BF16),
            pltpu.VMEM((2, 8, 2, 2, 128, 128), BF16),
            pltpu.VMEM((2, 128, 512), F32),
            dma(4), dma(4), dma(40), dma(40), dma(32), dma(2), dma(6), dma(9),
            dma(16), dma(1), dma(32),
        ],
        compiler_params=pltpu.CompilerParams(
            collective_id=0, has_side_effects=True, vmem_limit_bytes=56 * 2 ** 20),
        name="tile_attention",
    )(window_ext, tokens, w_qkv, w_out.T)


def solution(mesh):
    in_specs = (P("tile", None), P(None, "tile", "tensor"), P("tensor", "tile"), P("tensor", None))
    return jax.shard_map(
        per_device, mesh=mesh, in_specs=in_specs, out_specs=P("tile", "tensor"), check_vma=False)
```

```python
import functools

import jax
import jax.numpy as jnp
from jax import lax
from jax.experimental import pallas as pl
from jax.experimental.pallas import tpu as pltpu
from jax.sharding import PartitionSpec as P

MESH = pl.DeviceIdType.MESH
F32 = jnp.float32
BF16 = jnp.bfloat16
NZ = 16
ROUTE = ((1, 2), (1, 1), (1, 3), (1, 0), (0, 2), (0, 1), (0, 3), (0, 0))
SCALE = 128.0 ** -0.5


def kernel(win, tok_in, w_in, wo_in, out, tok, w, acc, kv, qs, mask, os, ts, attf, att, tmp, wo, fin, relay,
           s_tok, s_init, s_zp, s_zm, s_x, s_t, s_h, s_xe, s_wa, s_wc, s_ag, s_far):
    ti = lax.axis_index("tile")
    te = lax.axis_index("tensor")
    z, xl, c = ti // 4, (ti // 2) % 2, ti % 2
    xh, y = te // 4, te % 4
    t, h = z // 4, z % 4

    def at(z_, xl_, c_, xh_, y_):
        return (z_ * 4 + xl_ * 2 + c_, xh_ * 4 + y_)

    zn, zv = (z + 1) % NZ, (z + NZ - 1) % NZ
    mate = at(z, xl, 1 - c, xh, y)
    side = at(z, 1 - xl, c, xh, y)
    side_mate = at(z, 1 - xl, 1 - c, xh, y)
    z_next = at(zn, xl, c, xh, y)
    z_prev = at(zv, xl, c, xh, y)
    side_next = at(zn, 1 - xl, c, xh, y)
    side_prev = at(zv, 1 - xl, c, xh, y)
    later = at((z + 4) % NZ, xl, c, xh, y)
    earlier = at((z + NZ - 4) % NZ, xl, c, xh, y)
    six_up = at((z + 6) % NZ, xl, c, xh, y)
    six_down = at((z + NZ - 6) % NZ, xl, c, xh, y)

    def rc(src, dst, sems, i, dev):
        return pltpu.make_async_remote_copy(
            src_ref=src, dst_ref=dst, send_sem=sems.at[0, i], recv_sem=sems.at[1, i],
            device_id=dev, device_id_type=MESH)

    def rc2(src, dst, si, ri, sems, dev):
        return pltpu.make_async_remote_copy(
            src_ref=src, dst_ref=dst, send_sem=sems.at[0, si], recv_sem=sems.at[1, ri],
            device_id=dev, device_id_type=MESH)

    rows = pl.ds(pl.multiple_of(xl * 128, 128), 128)
    others = pl.ds(pl.multiple_of((1 - xl) * 128, 128), 128)
    r0 = pl.ds(pl.multiple_of(xl * 128 + c * 64, 64), 64)
    mine = pl.ds(pl.multiple_of(c * 128, 128), 128)
    theirs = pl.ds(pl.multiple_of((1 - c) * 128, 128), 128)

    own_w = pltpu.make_async_copy(w_in.at[:, :, mine], w.at[z, pl.ds(0, 3), r0, :], s_tok.at[0, 2])
    own_o = pltpu.make_async_copy(wo_in.at[:, mine], w.at[z, 3, r0, :], s_tok.at[0, 3])
    own_tok = pltpu.make_async_copy(tok_in, tok.at[c], s_tok.at[0, 1])
    for d in (own_w, own_o, own_tok):
        d.start()

    bar = pltpu.get_barrier_semaphore()

    def greet(dev):
        pl.semaphore_signal(bar, inc=1, device_id=dev, device_id_type=MESH)

    kv[...] = jnp.zeros_like(kv)
    for dev in (six_up, six_down, later, earlier, z_next, z_prev, side_next, side_prev, side_mate, mate):
        greet(dev)
    for dx in range(4):
        for dy in range(4):
            if dx or dy:
                greet(at(z, xl ^ (dx & 1), c, xh ^ (dx >> 1), (y + dy) % 4))
    for dx, dy in ((2, 0), (0, 1), (0, 2), (0, 3), (2, 1), (2, 2), (2, 3)):
        greet(at(z, xl, 1 - c, xh ^ (dx >> 1), (y + dy) % 4))
    pl.semaphore_wait(bar, 32)

    i_mate = rc(w_in.at[:, :, theirs], w.at[z, pl.ds(0, 3), r0, :], s_init, 0, mate)
    i_side = rc(w_in.at[0, :, mine], w.at[z, 0, r0, :], s_init, 1, side)
    i_diag = rc(w_in.at[0, :, theirs], w.at[z, 0, r0, :], s_init, 2, side_mate)
    i_out = rc(wo_in.at[:, theirs], w.at[z, 3, r0, :], s_init, 3, mate)
    i_mate.start()
    i_out.start()
    i_side.start()
    i_diag.start()
    tok_x = rc(tok_in, tok.at[c], s_tok, 0, mate)
    tok_x.start()

    def chunk(zo, ch):
        return w.at[zo, (1, 2, 0, 0, 3)[ch], others if ch == 3 else rows, :]

    def zp_copy(zo, ch, s):
        return rc(chunk(zo, ch), chunk(zo, ch), s_zp, ch * 8 + s, z_next)

    def zm_copy(zo, ch, s):
        return rc(chunk(zo, ch), chunk(zo, ch), s_zm, ch * 8 + s, z_prev)

    def x_copy(zo, m, i):
        return rc(chunk(zo, m), chunk(zo, m), s_x, m * 16 + i, side)

    own_w.wait()
    i_mate.wait_recv()
    for ch in range(2):
        zp_copy(z, ch, 0).start()
        zm_copy(z, ch, 0).start()
        x_copy(z, ch, 0).start()
    zp_copy(z, 2, 0).start()
    zm_copy(z, 2, 0).start()
    own_o.wait()
    i_out.wait_recv()
    i_side.wait_recv()
    i_diag.wait_recv()
    for ch in (3, 4):
        zp_copy(z, ch, 0).start()
        zm_copy(z, ch, 0).start()

    rh, rw, rt = win[c, 1], win[c, 2], win[c, 0]
    qi = lax.broadcasted_iota(jnp.int32, (64, 384), 0)
    ki = lax.broadcasted_iota(jnp.int32, (64, 384), 1)
    grp = ki // 128
    krow = (ki % 128) // 8
    d_r = jnp.abs(krow - 4 - qi // 8)
    d_c = jnp.abs((grp - 1) * 8 + ki % 8 - qi % 8)
    grow = h * 8 + krow - 4
    near = (d_r <= rh) & (d_c <= rw) & (grow >= 0) & (grow < 32)
    for u in range(4):
        gcol = xl * 4 + u + grp - 1
        mask[u] = jnp.where(near & (gcol >= 0) & (gcol < 8), F32(1.0), F32(0.0))

    def allow(a, f):
        df = 2 + a - f
        ok = jnp.where(rt >= df, F32(1.0), F32(0.0))
        if f < 2:
            ok = jnp.where(t > 0, ok, F32(0.0))
        return ok

    def project(zo):
        cols = pl.ds(pl.multiple_of(zo * 256, 256), 256)
        lhs = tok[:, :, cols].reshape(512, 256)
        rhs = jnp.concatenate([w[zo, 0], w[zo, 1], w[zo, 2]], axis=1)
        return jnp.dot(lhs, rhs, preferred_element_type=F32)

    def take(s, ch):
        zp, zm = (z + NZ - s) % NZ, (z + s) % NZ
        last_p, last_m = (8, 7) if ch in (2, 3) else (7, 8)

        @pl.when(s <= last_p)
        def _():
            zp_copy(zp, ch, s - 1).wait_recv()

            @pl.when(s < last_p)
            def _():
                zp_copy(zp, ch, s).start()
            if ch < 2:
                x_copy(zp, ch, s).start()

        @pl.when(s <= last_m)
        def _():
            zm_copy(zm, ch, s - 1).wait_recv()

            @pl.when(s < last_m)
            def _():
                zm_copy(zm, ch, s).start()
            if ch < 2:
                x_copy(zm, ch, 7 + s).start()

    def both_sides(s):
        zq = (z + NZ - s) % NZ
        x_copy(zq, 0, s).wait_recv()
        x_copy(zq, 1, s).wait_recv()
        acc[...] += project(zq)
        zr = (z + s) % NZ
        x_copy(zr, 0, 7 + s).wait_recv()
        x_copy(zr, 1, 7 + s).wait_recv()
        acc[...] += project(zr)

    def fwd(s, _):
        for ch in range(5):
            take(s, ch)

        @pl.when(s == 1)
        def _():
            own_tok.wait()
            tok_x.wait_recv()
            x_copy(z, 0, 0).wait_recv()
            x_copy(z, 1, 0).wait_recv()
            acc[...] = project(z)

        @pl.when(s > 1)
        def _():
            both_sides(s - 1)
        return 0

    lax.fori_loop(1, 8, fwd, 0)
    take(8, 0)
    take(8, 1)
    both_sides(7)
    z8 = (z + 8) % NZ
    x_copy(z8, 0, 15).wait_recv()
    x_copy(z8, 1, 15).wait_recv()
    lhs8 = tok[:, :, pl.ds(pl.multiple_of(z8 * 256, 256), 256)].reshape(512, 256)
    acc[:, 128:384] += jnp.dot(lhs8, jnp.concatenate([w[z8, 1], w[z8, 2]], axis=1), preferred_element_type=F32)

    def unit(p):
        return p * lax.rsqrt(jnp.mean(p * p, axis=-1, keepdims=True) + 1e-06)

    for tw in range(2):
        for a in range(2):
            at_rows = pl.ds(tw * 256 + a * 128, 128)
            both = jnp.concatenate([unit(acc[at_rows, 128:256]), acc[at_rows, 256:384]], axis=1)
            both = both.reshape(8, 2, 8, 256)
            for g in range(2):
                kv[2 + a, 1 + tw * 2 + g, 32:96, :] = both[:, g].reshape(64, 256).astype(BF16)

    edge_out = 4 - 3 * xl
    edge_in = 5 * xl
    OWN, TOP, BOT = pl.ds(32, 64), pl.ds(0, 32), pl.ds(96, 32)
    UP, DOWN = pl.ds(32, 32), pl.ds(64, 32)
    MIDG = pl.ds(1, 4)
    FRAMES = (pl.ds(2, 2), pl.ds(1, 1), pl.ds(0, 1))

    def t_halo(f):
        grp = MIDG if f else pl.ds(1, 3)
        return rc(kv.at[2 + f, grp, OWN, :], kv.at[f, grp, OWN, :], s_t, f, later)

    far_1 = rc(kv.at[2, 4, OWN, :], relay, s_far, 0, six_down)
    far_2 = rc(relay, kv.at[0, 4, OWN, :], s_far, 1, six_down)
    has_relay = (z + 6) % NZ < 12

    def h_down(i):
        return rc(kv.at[FRAMES[i], MIDG, DOWN, :], kv.at[FRAMES[i], MIDG, TOP, :], s_h, i, z_next)

    def h_up(i):
        return rc(kv.at[FRAMES[i], MIDG, UP, :], kv.at[FRAMES[i], MIDG, BOT, :], s_h, 3 + i, z_prev)

    def x_own(i):
        return rc(kv.at[FRAMES[i], edge_out, OWN, :], kv.at[FRAMES[i], edge_in, OWN, :], s_xe, i, side)

    def x_down(i):
        return rc(kv.at[FRAMES[i], edge_out, DOWN, :], kv.at[FRAMES[i], edge_in, TOP, :], s_xe, 3 + i, side_next)

    def x_up(i):
        return rc(kv.at[FRAMES[i], edge_out, UP, :], kv.at[FRAMES[i], edge_in, BOT, :], s_xe, 6 + i, side_prev)

    has_prev, has_later = t > 0, t < 3
    has_up, has_down = h > 0, h < 3

    def halo_start(i):
        @pl.when(has_down)
        def _():
            h_down(i).start()
            x_down(i).start()

        @pl.when(has_up)
        def _():
            h_up(i).start()
            x_up(i).start()
        x_own(i).start()

    def halo_wait(i):
        x_own(i).wait_recv()

        @pl.when(has_up)
        def _():
            h_down(i).wait_recv()
            x_down(i).wait_recv()

        @pl.when(has_down)
        def _():
            h_up(i).wait_recv()
            x_up(i).wait_recv()

    def halo_sent(i):
        x_own(i).wait_send()

        @pl.when(has_down)
        def _():
            h_down(i).wait_send()
            x_down(i).wait_send()

        @pl.when(has_up)
        def _():
            h_up(i).wait_send()
            x_up(i).wait_send()

    @pl.when(has_later)
    def _():
        far_1.start()
        t_halo(1).start()
    halo_start(0)

    for ch in (2, 3, 4):
        take(8, ch)

    def wa(dx, dy):
        xh2, y2 = xh ^ (dx >> 1), (y + dy) % 4
        j2 = xh2 * 4 + y2
        src = w.at[pl.ds(2 * j2, 2), 3, rows, :]
        return rc(src, wo.at[c, xh * 4 + y, xl], s_wa, dx * 4 + dy, at(z, xl ^ (dx & 1), c, xh2, y2))

    for dx in range(4):
        for dy in range(4):
            if dx or dy:
                wa(dx, dy).start()
    own_wo = pltpu.make_async_copy(w.at[pl.ds(2 * te, 2), 3, rows, :], wo.at[c, te, xl], s_wa.at[0, 0])
    own_wo.start()

    acc[:, 0:128] += jnp.dot(
        tok[:, :, pl.ds(pl.multiple_of(z8 * 256, 256), 256)].reshape(512, 256), w[z8, 0], preferred_element_type=F32)
    for tw in range(2):
        for a in range(2):
            q = unit(acc[pl.ds(tw * 256 + a * 128, 128), 0:128]).reshape(8, 2, 8, 128)
            for g in range(2):
                qs[tw * 2 + g, a] = q[:, g].reshape(64, 128).astype(BF16)

    def attend(u, a, f):
        keys = kv[f, u:u + 3, :, 0:128].reshape(384, 128)
        vals = kv[f, u:u + 3, :, 128:256].reshape(384, 128)
        s = lax.dot_general(qs[u, a], keys, (((1,), (1,)), ((), ())), preferred_element_type=F32)
        wt = jnp.exp(s * SCALE) * (mask[u] * allow(a, f))
        part = wt[:, 0:128] + wt[:, 128:256] + wt[:, 256:384]
        return jnp.dot(wt.astype(BF16), vals, preferred_element_type=F32), part

    halo_wait(0)
    for u in range(4):
        o, p = attend(u, 0, 2)
        os[u, 0] = o
        ts[u, 0] = p
        o2, p2 = attend(u, 1, 2)
        o3, p3 = attend(u, 1, 3)
        os[u, 1] = o2 + o3
        ts[u, 1] = p2 + p3

    @pl.when(has_later)
    def _():
        t_halo(0).start()

    te_x = (1 - xh) * 4 + y

    def slot(a, k, dy, p):
        return ((a * 2 + k) * 4 + dy) * 2 + p

    def a_out(a, k, dy, own):
        src = att.at[te, c, a] if own else tmp.at[1 - c, a]
        dev = at(z, xl, c if own else 1 - c, 1 - xh if k else xh, (y + dy) % 4)
        return rc2(src, att.at[te, c, a], slot(a, k, dy, 0 if own else 1), slot(a, k, dy, c), s_ag, dev)

    def a_in(a, k, dy, p):
        return rc(att.at[te, p, a], att.at[te, p, a], s_ag, slot(a, k, dy, p), mate)

    def finish(a, f):
        for u in range(4):
            o, p = attend(u, a, f)
            total = jnp.sum(ts[u, a] + p, axis=-1, keepdims=True)
            res = (os[u, a] + o) / total
            attf[u // 2, :, u % 2] = res.reshape(8, 8, 128)
        for tw in range(2):
            tmp[tw, a] = attf[tw].reshape(128, 128).astype(BF16)
        att[te, c, a] = tmp[c, a]
        for k, dy in ROUTE:
            if k or dy:
                a_out(a, k, dy, True).start()
            a_out(a, k, dy, False).start()

    def term(j, a):
        lhs = jnp.concatenate([att[j, 0, a], att[j, 1, a]], axis=1)
        rhs = jnp.concatenate([
            jnp.concatenate([wo[0, j, x, k], wo[1, j, x, k]], axis=1)
            for k in range(2) for x in range(2)], axis=0)
        return lax.dot_general(lhs, rhs, (((1,), (1,)), ((), ())), preferred_element_type=F32)

    def mix(a):
        tot = fin.at[a]
        for k, dy in ROUTE[::-1]:
            if k or dy:
                a_in(a, k, dy, 0).wait_recv()
                a_in(a, k, dy, 1).wait_recv()
                xs = 1 - xh if k else xh
                tot[...] += term(xs * 4 + (y + 4 - dy) % 4, a)
            else:
                rc2(att.at[te, 0, a], att.at[te, 0, a], 0, slot(a, 0, 0, 1 - c), s_ag, mate).wait_recv()
                tot[...] = term(te, a)
        out[a * 128:(a + 1) * 128, :] = tot[...].astype(BF16)

    @pl.when(has_prev)
    def _():
        t_halo(1).wait_recv()
        halo_start(1)

    @pl.when(has_relay)
    def _():
        far_1.wait_recv()
        far_2.start()

    @pl.when(has_prev)
    def _():
        halo_wait(1)
    finish(1, 1)

    for u in range(4):
        o, p = attend(u, 0, 1)
        os[u, 0] += o
        ts[u, 0] += p
    own_wo.wait()
    for dx in range(4):
        for dy in range(4):
            if dx or dy:
                wa(dx, dy).wait_recv()
    wo_x = rc(wo.at[c], wo.at[c], s_wc, 0, mate)
    wo_x.start()

    @pl.when(has_prev)
    def _():
        t_halo(0).wait_recv()
        far_2.wait_recv()
        halo_start(2)

    @pl.when(has_prev)
    def _():
        halo_wait(2)
    finish(0, 0)
    wo_x.wait_recv()
    mix(1)
    mix(0)

    for d in (i_mate, i_side, i_diag, i_out, tok_x, wo_x):
        d.wait_send()

    def drain(s, _):
        for m in range(2):
            x_copy(z, m, s).wait_send()

        @pl.when(s < 8)
        def _():
            for ch in range(5):
                (zp_copy if ch in (2, 3) else zm_copy)(z, ch, s).wait_send()

        @pl.when(s < 7)
        def _():
            for ch in range(5):
                (zm_copy if ch in (2, 3) else zp_copy)(z, ch, s).wait_send()
        return 0

    lax.fori_loop(0, 16, drain, 0)
    for dx in range(4):
        for dy in range(4):
            if dx or dy:
                wa(dx, dy).wait_send()
    for a in range(2):
        for k, dy in ROUTE:
            if k or dy:
                a_out(a, k, dy, True).wait_send()
            a_out(a, k, dy, False).wait_send()
    halo_sent(0)

    @pl.when(has_later)
    def _():
        t_halo(0).wait_send()
        t_halo(1).wait_send()
        far_1.wait_send()

    @pl.when(has_relay)
    def _():
        far_2.wait_send()

    @pl.when(has_prev)
    def _():
        halo_sent(1)
        halo_sent(2)


def per_device(tokens, w_qkv, w_out, window_ext):
    vm = pl.BlockSpec(memory_space=pltpu.VMEM)
    hbm = pl.BlockSpec(memory_space=pl.ANY)
    dma = lambda n: pltpu.SemaphoreType.DMA((2, n))
    return pl.pallas_call(
        kernel,
        out_shape=jax.ShapeDtypeStruct((256, 512), BF16),
        in_specs=[pl.BlockSpec(memory_space=pltpu.SMEM), hbm, hbm, hbm],
        out_specs=vm,
        scratch_shapes=[
            pltpu.VMEM((2, 256, 4096), BF16),
            pltpu.VMEM((16, 4, 256, 128), BF16),
            pltpu.VMEM((512, 384), F32),
            pltpu.VMEM((4, 6, 128, 256), BF16),
            pltpu.VMEM((4, 2, 64, 128), BF16),
            pltpu.VMEM((4, 64, 384), F32),
            pltpu.VMEM((4, 2, 64, 128), F32),
            pltpu.VMEM((4, 2, 64, 128), F32),
            pltpu.VMEM((2, 8, 2, 8, 128), F32),
            pltpu.VMEM((8, 2, 2, 128, 128), BF16),
            pltpu.VMEM((2, 2, 128, 128), BF16),
            pltpu.VMEM((2, 8, 2, 2, 128, 128), BF16),
            pltpu.VMEM((2, 128, 512), F32),
            pltpu.VMEM((64, 256), BF16),
            dma(4), dma(4), dma(40), dma(40), dma(32), dma(2), dma(6), dma(9),
            dma(16), dma(1), dma(32), dma(2),
        ],
        compiler_params=pltpu.CompilerParams(
            collective_id=0, has_side_effects=True, vmem_limit_bytes=56 * 2 ** 20),
        name="tile_attention",
    )(window_ext, tokens, w_qkv, w_out.T)


def solution(mesh):
    in_specs = (P("tile", None), P(None, "tile", "tensor"), P("tensor", "tile"), P("tensor", None))
    return jax.shard_map(
        per_device, mesh=mesh, in_specs=in_specs, out_specs=P("tile", "tensor"), check_vma=False)
```

```python
import functools

import jax
import jax.numpy as jnp
from jax import lax
from jax.experimental import pallas as pl
from jax.experimental.pallas import tpu as pltpu
from jax.sharding import PartitionSpec as P

MESH = pl.DeviceIdType.MESH
F32 = jnp.float32
BF16 = jnp.bfloat16
NZ = 16
ROUTE = ((1, 2), (1, 1), (1, 3), (1, 0), (0, 2), (0, 1), (0, 3), (0, 0))
SCALE = 128.0 ** -0.5


def kernel(win, tok_in, w_in, wo_in, out, tok, w, acc, kv, qs, mask, os, ts, attf, att, tmp, wo, fin, relay,
           s_tok, s_init, s_zp, s_zm, s_x, s_t, s_h, s_xe, s_wa, s_wc, s_ag, s_far):
    ti = lax.axis_index("tile")
    te = lax.axis_index("tensor")
    z, xl, c = ti // 4, (ti // 2) % 2, ti % 2
    xh, y = te // 4, te % 4
    t, h = z // 4, z % 4

    def at(z_, xl_, c_, xh_, y_):
        return (z_ * 4 + xl_ * 2 + c_, xh_ * 4 + y_)

    zn, zv = (z + 1) % NZ, (z + NZ - 1) % NZ
    mate = at(z, xl, 1 - c, xh, y)
    side = at(z, 1 - xl, c, xh, y)
    side_mate = at(z, 1 - xl, 1 - c, xh, y)
    z_next = at(zn, xl, c, xh, y)
    z_prev = at(zv, xl, c, xh, y)
    side_next = at(zn, 1 - xl, c, xh, y)
    side_prev = at(zv, 1 - xl, c, xh, y)
    later = at((z + 4) % NZ, xl, c, xh, y)
    earlier = at((z + NZ - 4) % NZ, xl, c, xh, y)
    six_up = at((z + 6) % NZ, xl, c, xh, y)
    six_down = at((z + NZ - 6) % NZ, xl, c, xh, y)

    def rc(src, dst, sems, i, dev):
        return pltpu.make_async_remote_copy(
            src_ref=src, dst_ref=dst, send_sem=sems.at[0, i], recv_sem=sems.at[1, i],
            device_id=dev, device_id_type=MESH)

    def rc2(src, dst, si, ri, sems, dev):
        return pltpu.make_async_remote_copy(
            src_ref=src, dst_ref=dst, send_sem=sems.at[0, si], recv_sem=sems.at[1, ri],
            device_id=dev, device_id_type=MESH)

    rows = pl.ds(pl.multiple_of(xl * 128, 128), 128)
    others = pl.ds(pl.multiple_of((1 - xl) * 128, 128), 128)
    r0 = pl.ds(pl.multiple_of(xl * 128 + c * 64, 64), 64)
    mine = pl.ds(pl.multiple_of(c * 128, 128), 128)
    theirs = pl.ds(pl.multiple_of((1 - c) * 128, 128), 128)

    own_w = pltpu.make_async_copy(w_in.at[:, :, mine], w.at[z, pl.ds(0, 3), r0, :], s_tok.at[0, 2])
    own_o = pltpu.make_async_copy(wo_in.at[:, mine], w.at[z, 3, r0, :], s_tok.at[0, 3])
    own_tok = pltpu.make_async_copy(tok_in, tok.at[c], s_tok.at[0, 1])
    for d in (own_w, own_o, own_tok):
        d.start()

    bar = pltpu.get_barrier_semaphore()

    def greet(dev):
        pl.semaphore_signal(bar, inc=1, device_id=dev, device_id_type=MESH)

    kv[...] = jnp.zeros_like(kv)
    for dev in (six_up, six_down, later, earlier, z_next, z_prev, side_next, side_prev, side_mate, mate):
        greet(dev)
    for dx in range(4):
        for dy in range(4):
            if dx or dy:
                greet(at(z, xl ^ (dx & 1), c, xh ^ (dx >> 1), (y + dy) % 4))
    for dx, dy in ((2, 0), (0, 1), (0, 2), (0, 3), (2, 1), (2, 2), (2, 3)):
        greet(at(z, xl, 1 - c, xh ^ (dx >> 1), (y + dy) % 4))
    pl.semaphore_wait(bar, 32)

    i_mate = rc(w_in.at[:, :, theirs], w.at[z, pl.ds(0, 3), r0, :], s_init, 0, mate)
    i_side = rc(w_in.at[0, :, mine], w.at[z, 0, r0, :], s_init, 1, side)
    i_diag = rc(w_in.at[0, :, theirs], w.at[z, 0, r0, :], s_init, 2, side_mate)
    i_out = rc(wo_in.at[:, theirs], w.at[z, 3, r0, :], s_init, 3, mate)
    i_mate.start()
    i_out.start()
    i_side.start()
    i_diag.start()
    tok_x = rc(tok_in, tok.at[c], s_tok, 0, mate)
    tok_x.start()

    def chunk(zo, ch):
        return w.at[zo, (1, 2, 0, 0, 3)[ch], others if ch == 3 else rows, :]

    def zp_copy(zo, ch, s):
        return rc(chunk(zo, ch), chunk(zo, ch), s_zp, ch * 8 + s, z_next)

    def zm_copy(zo, ch, s):
        return rc(chunk(zo, ch), chunk(zo, ch), s_zm, ch * 8 + s, z_prev)

    def x_copy(zo, m, i):
        return rc(chunk(zo, m), chunk(zo, m), s_x, m * 16 + i, side)

    own_w.wait()
    i_mate.wait_recv()
    for ch in range(2):
        zp_copy(z, ch, 0).start()
        zm_copy(z, ch, 0).start()
        x_copy(z, ch, 0).start()
    zp_copy(z, 2, 0).start()
    zm_copy(z, 2, 0).start()
    own_o.wait()
    i_out.wait_recv()
    i_side.wait_recv()
    i_diag.wait_recv()
    for ch in (3, 4):
        zp_copy(z, ch, 0).start()
        zm_copy(z, ch, 0).start()

    rh, rw, rt = win[c, 1], win[c, 2], win[c, 0]
    qi = lax.broadcasted_iota(jnp.int32, (64, 384), 0)
    ki = lax.broadcasted_iota(jnp.int32, (64, 384), 1)
    grp = ki // 128
    krow = (ki % 128) // 8
    d_r = jnp.abs(krow - 4 - qi // 8)
    d_c = jnp.abs((grp - 1) * 8 + ki % 8 - qi % 8)
    grow = h * 8 + krow - 4
    near = (d_r <= rh) & (d_c <= rw) & (grow >= 0) & (grow < 32)
    for u in range(4):
        gcol = xl * 4 + u + grp - 1
        mask[u] = jnp.where(near & (gcol >= 0) & (gcol < 8), F32(1.0), F32(0.0))

    def allow(a, f):
        df = 2 + a - f
        ok = jnp.where(rt >= df, F32(1.0), F32(0.0))
        if f < 2:
            ok = jnp.where(t > 0, ok, F32(0.0))
        return ok

    def project(zo):
        cols = pl.ds(pl.multiple_of(zo * 256, 256), 256)
        lhs = tok[:, :, cols].reshape(512, 256)
        rhs = jnp.concatenate([w[zo, 0], w[zo, 1], w[zo, 2]], axis=1)
        return jnp.dot(lhs, rhs, preferred_element_type=F32)

    def take(s, ch):
        zp, zm = (z + NZ - s) % NZ, (z + s) % NZ
        last_p, last_m = (8, 7) if ch in (2, 3) else (7, 8)

        @pl.when(s <= last_p)
        def _():
            zp_copy(zp, ch, s - 1).wait_recv()

            @pl.when(s < last_p)
            def _():
                zp_copy(zp, ch, s).start()
            if ch < 2:
                x_copy(zp, ch, s).start()

        @pl.when(s <= last_m)
        def _():
            zm_copy(zm, ch, s - 1).wait_recv()

            @pl.when(s < last_m)
            def _():
                zm_copy(zm, ch, s).start()
            if ch < 2:
                x_copy(zm, ch, 7 + s).start()

    def both_sides(s):
        zq = (z + NZ - s) % NZ
        x_copy(zq, 0, s).wait_recv()
        x_copy(zq, 1, s).wait_recv()
        acc[...] += project(zq)
        zr = (z + s) % NZ
        x_copy(zr, 0, 7 + s).wait_recv()
        x_copy(zr, 1, 7 + s).wait_recv()
        acc[...] += project(zr)

    def fwd(s, _):
        for ch in range(5):
            take(s, ch)

        @pl.when(s == 1)
        def _():
            own_tok.wait()
            tok_x.wait_recv()
            x_copy(z, 0, 0).wait_recv()
            x_copy(z, 1, 0).wait_recv()
            acc[...] = project(z)

        @pl.when(s > 1)
        def _():
            both_sides(s - 1)
        return 0

    lax.fori_loop(1, 8, fwd, 0)
    take(8, 0)
    take(8, 1)
    both_sides(7)
    z8 = (z + 8) % NZ
    x_copy(z8, 0, 15).wait_recv()
    x_copy(z8, 1, 15).wait_recv()
    lhs8 = tok[:, :, pl.ds(pl.multiple_of(z8 * 256, 256), 256)].reshape(512, 256)
    acc[:, 128:384] += jnp.dot(lhs8, jnp.concatenate([w[z8, 1], w[z8, 2]], axis=1), preferred_element_type=F32)

    def unit(p):
        return p * lax.rsqrt(jnp.mean(p * p, axis=-1, keepdims=True) + 1e-06)

    for tw in range(2):
        for a in range(2):
            at_rows = pl.ds(tw * 256 + a * 128, 128)
            both = jnp.concatenate([unit(acc[at_rows, 128:256]), acc[at_rows, 256:384]], axis=1)
            both = both.reshape(8, 2, 8, 256)
            for g in range(2):
                kv[2 + a, 1 + tw * 2 + g, 32:96, :] = both[:, g].reshape(64, 256).astype(BF16)

    edge_out = 4 - 3 * xl
    edge_in = 5 * xl
    OWN, TOP, BOT = pl.ds(32, 64), pl.ds(0, 32), pl.ds(96, 32)
    UP, DOWN = pl.ds(32, 32), pl.ds(64, 32)
    MIDG = pl.ds(1, 4)
    FRAMES = (pl.ds(2, 2), pl.ds(1, 1), pl.ds(0, 1))

    def t_halo(f):
        grp = MIDG if f else pl.ds(1, 2)
        return rc(kv.at[2 + f, grp, OWN, :], kv.at[f, grp, OWN, :], s_t, f, later)

    far_1 = rc(kv.at[2, pl.ds(3, 2), OWN, :], relay, s_far, 0, six_down)
    far_2 = rc(relay, kv.at[0, pl.ds(3, 2), OWN, :], s_far, 1, six_down)
    has_relay = (z + 6) % NZ < 12

    def h_down(i):
        return rc(kv.at[FRAMES[i], MIDG, DOWN, :], kv.at[FRAMES[i], MIDG, TOP, :], s_h, i, z_next)

    def h_up(i):
        return rc(kv.at[FRAMES[i], MIDG, UP, :], kv.at[FRAMES[i], MIDG, BOT, :], s_h, 3 + i, z_prev)

    def x_own(i):
        return rc(kv.at[FRAMES[i], edge_out, OWN, :], kv.at[FRAMES[i], edge_in, OWN, :], s_xe, i, side)

    def x_down(i):
        return rc(kv.at[FRAMES[i], edge_out, DOWN, :], kv.at[FRAMES[i], edge_in, TOP, :], s_xe, 3 + i, side_next)

    def x_up(i):
        return rc(kv.at[FRAMES[i], edge_out, UP, :], kv.at[FRAMES[i], edge_in, BOT, :], s_xe, 6 + i, side_prev)

    has_prev, has_later = t > 0, t < 3
    has_up, has_down = h > 0, h < 3

    def halo_start(i):
        @pl.when(has_down)
        def _():
            h_down(i).start()
            x_down(i).start()

        @pl.when(has_up)
        def _():
            h_up(i).start()
            x_up(i).start()
        x_own(i).start()

    def halo_wait(i):
        x_own(i).wait_recv()

        @pl.when(has_up)
        def _():
            h_down(i).wait_recv()
            x_down(i).wait_recv()

        @pl.when(has_down)
        def _():
            h_up(i).wait_recv()
            x_up(i).wait_recv()

    def halo_sent(i):
        x_own(i).wait_send()

        @pl.when(has_down)
        def _():
            h_down(i).wait_send()
            x_down(i).wait_send()

        @pl.when(has_up)
        def _():
            h_up(i).wait_send()
            x_up(i).wait_send()

    @pl.when(has_later)
    def _():
        far_1.start()
        t_halo(1).start()
    halo_start(0)

    for ch in (2, 3, 4):
        take(8, ch)

    def wa(dx, dy):
        xh2, y2 = xh ^ (dx >> 1), (y + dy) % 4
        j2 = xh2 * 4 + y2
        src = w.at[pl.ds(2 * j2, 2), 3, rows, :]
        return rc(src, wo.at[c, xh * 4 + y, xl], s_wa, dx * 4 + dy, at(z, xl ^ (dx & 1), c, xh2, y2))

    for dx in range(4):
        for dy in range(4):
            if dx or dy:
                wa(dx, dy).start()
    own_wo = pltpu.make_async_copy(w.at[pl.ds(2 * te, 2), 3, rows, :], wo.at[c, te, xl], s_wa.at[0, 0])
    own_wo.start()

    acc[:, 0:128] += jnp.dot(
        tok[:, :, pl.ds(pl.multiple_of(z8 * 256, 256), 256)].reshape(512, 256), w[z8, 0], preferred_element_type=F32)
    for tw in range(2):
        for a in range(2):
            q = unit(acc[pl.ds(tw * 256 + a * 128, 128), 0:128]).reshape(8, 2, 8, 128)
            for g in range(2):
                qs[tw * 2 + g, a] = q[:, g].reshape(64, 128).astype(BF16)

    def attend(u, a, f):
        keys = kv[f, u:u + 3, :, 0:128].reshape(384, 128)
        vals = kv[f, u:u + 3, :, 128:256].reshape(384, 128)
        s = lax.dot_general(qs[u, a], keys, (((1,), (1,)), ((), ())), preferred_element_type=F32)
        wt = jnp.exp(s * SCALE) * (mask[u] * allow(a, f))
        part = wt[:, 0:128] + wt[:, 128:256] + wt[:, 256:384]
        return jnp.dot(wt.astype(BF16), vals, preferred_element_type=F32), part

    halo_wait(0)
    for u in range(4):
        o, p = attend(u, 0, 2)
        os[u, 0] = o
        ts[u, 0] = p
        o2, p2 = attend(u, 1, 2)
        o3, p3 = attend(u, 1, 3)
        os[u, 1] = o2 + o3
        ts[u, 1] = p2 + p3

    @pl.when(has_later)
    def _():
        t_halo(0).start()

    te_x = (1 - xh) * 4 + y

    def slot(a, k, dy, p):
        return ((a * 2 + k) * 4 + dy) * 2 + p

    def a_out(a, k, dy, own):
        src = att.at[te, c, a] if own else tmp.at[1 - c, a]
        dev = at(z, xl, c if own else 1 - c, 1 - xh if k else xh, (y + dy) % 4)
        return rc2(src, att.at[te, c, a], slot(a, k, dy, 0 if own else 1), slot(a, k, dy, c), s_ag, dev)

    def a_in(a, k, dy, p):
        return rc(att.at[te, p, a], att.at[te, p, a], s_ag, slot(a, k, dy, p), mate)

    def finish(a, f):
        for u in range(4):
            o, p = attend(u, a, f)
            total = jnp.sum(ts[u, a] + p, axis=-1, keepdims=True)
            res = (os[u, a] + o) / total
            attf[u // 2, :, u % 2] = res.reshape(8, 8, 128)
        for tw in range(2):
            tmp[tw, a] = attf[tw].reshape(128, 128).astype(BF16)
        att[te, c, a] = tmp[c, a]
        for k, dy in ROUTE:
            if k or dy:
                a_out(a, k, dy, True).start()
            a_out(a, k, dy, False).start()

    def term(j, a):
        lhs = jnp.concatenate([att[j, 0, a], att[j, 1, a]], axis=1)
        rhs = jnp.concatenate([
            jnp.concatenate([wo[0, j, x, k], wo[1, j, x, k]], axis=1)
            for k in range(2) for x in range(2)], axis=0)
        return lax.dot_general(lhs, rhs, (((1,), (1,)), ((), ())), preferred_element_type=F32)

    def mix(a):
        tot = fin.at[a]
        for k, dy in ROUTE[::-1]:
            if k or dy:
                a_in(a, k, dy, 0).wait_recv()
                a_in(a, k, dy, 1).wait_recv()
                xs = 1 - xh if k else xh
                tot[...] += term(xs * 4 + (y + 4 - dy) % 4, a)
            else:
                rc2(att.at[te, 0, a], att.at[te, 0, a], 0, slot(a, 0, 0, 1 - c), s_ag, mate).wait_recv()
                tot[...] = term(te, a)
        out[a * 128:(a + 1) * 128, :] = tot[...].astype(BF16)

    @pl.when(has_prev)
    def _():
        t_halo(1).wait_recv()
        halo_start(1)

    @pl.when(has_relay)
    def _():
        far_1.wait_recv()
        far_2.start()

    @pl.when(has_prev)
    def _():
        halo_wait(1)
    finish(1, 1)

    for u in range(4):
        o, p = attend(u, 0, 1)
        os[u, 0] += o
        ts[u, 0] += p
    own_wo.wait()
    for dx in range(4):
        for dy in range(4):
            if dx or dy:
                wa(dx, dy).wait_recv()
    wo_x = rc(wo.at[c], wo.at[c], s_wc, 0, mate)
    wo_x.start()

    @pl.when(has_prev)
    def _():
        t_halo(0).wait_recv()
        far_2.wait_recv()
        halo_start(2)

    @pl.when(has_prev)
    def _():
        halo_wait(2)
    finish(0, 0)
    wo_x.wait_recv()
    mix(1)
    mix(0)

    for d in (i_mate, i_side, i_diag, i_out, tok_x, wo_x):
        d.wait_send()

    def drain(s, _):
        for m in range(2):
            x_copy(z, m, s).wait_send()

        @pl.when(s < 8)
        def _():
            for ch in range(5):
                (zp_copy if ch in (2, 3) else zm_copy)(z, ch, s).wait_send()

        @pl.when(s < 7)
        def _():
            for ch in range(5):
                (zm_copy if ch in (2, 3) else zp_copy)(z, ch, s).wait_send()
        return 0

    lax.fori_loop(0, 16, drain, 0)
    for dx in range(4):
        for dy in range(4):
            if dx or dy:
                wa(dx, dy).wait_send()
    for a in range(2):
        for k, dy in ROUTE:
            if k or dy:
                a_out(a, k, dy, True).wait_send()
            a_out(a, k, dy, False).wait_send()
    halo_sent(0)

    @pl.when(has_later)
    def _():
        t_halo(0).wait_send()
        t_halo(1).wait_send()
        far_1.wait_send()

    @pl.when(has_relay)
    def _():
        far_2.wait_send()

    @pl.when(has_prev)
    def _():
        halo_sent(1)
        halo_sent(2)


def per_device(tokens, w_qkv, w_out, window_ext):
    vm = pl.BlockSpec(memory_space=pltpu.VMEM)
    hbm = pl.BlockSpec(memory_space=pl.ANY)
    dma = lambda n: pltpu.SemaphoreType.DMA((2, n))
    return pl.pallas_call(
        kernel,
        out_shape=jax.ShapeDtypeStruct((256, 512), BF16),
        in_specs=[pl.BlockSpec(memory_space=pltpu.SMEM), hbm, hbm, hbm],
        out_specs=vm,
        scratch_shapes=[
            pltpu.VMEM((2, 256, 4096), BF16),
            pltpu.VMEM((16, 4, 256, 128), BF16),
            pltpu.VMEM((512, 384), F32),
            pltpu.VMEM((4, 6, 128, 256), BF16),
            pltpu.VMEM((4, 2, 64, 128), BF16),
            pltpu.VMEM((4, 64, 384), F32),
            pltpu.VMEM((4, 2, 64, 128), F32),
            pltpu.VMEM((4, 2, 64, 128), F32),
            pltpu.VMEM((2, 8, 2, 8, 128), F32),
            pltpu.VMEM((8, 2, 2, 128, 128), BF16),
            pltpu.VMEM((2, 2, 128, 128), BF16),
            pltpu.VMEM((2, 8, 2, 2, 128, 128), BF16),
            pltpu.VMEM((2, 128, 512), F32),
            pltpu.VMEM((2, 64, 256), BF16),
            dma(4), dma(4), dma(40), dma(40), dma(32), dma(2), dma(6), dma(9),
            dma(16), dma(1), dma(32), dma(2),
        ],
        compiler_params=pltpu.CompilerParams(
            collective_id=0, has_side_effects=True, vmem_limit_bytes=56 * 2 ** 20),
        name="tile_attention",
    )(window_ext, tokens, w_qkv, w_out.T)


def solution(mesh):
    in_specs = (P("tile", None), P(None, "tile", "tensor"), P("tensor", "tile"), P("tensor", None))
    return jax.shard_map(
        per_device, mesh=mesh, in_specs=in_specs, out_specs=P("tile", "tensor"), check_vma=False)
```

```python
import functools

import jax
import jax.numpy as jnp
from jax import lax
from jax.experimental import pallas as pl
from jax.experimental.pallas import tpu as pltpu
from jax.sharding import PartitionSpec as P

MESH = pl.DeviceIdType.MESH
F32 = jnp.float32
BF16 = jnp.bfloat16
NZ = 16
ROUTE = ((1, 2), (1, 1), (1, 3), (1, 0), (0, 2), (0, 1), (0, 3), (0, 0))
SCALE = 128.0 ** -0.5


def kernel(win, tok_in, w_in, wo_in, out, tok, w, acc, kv, qs, mask, os, ts, attf, att, tmp, wo, fin, relay,
           s_tok, s_init, s_zp, s_zm, s_x, s_t, s_h, s_xe, s_wa, s_wc, s_ag, s_far):
    ti = lax.axis_index("tile")
    te = lax.axis_index("tensor")
    z, xl, c = ti // 4, (ti // 2) % 2, ti % 2
    xh, y = te // 4, te % 4
    t, h = z // 4, z % 4

    def at(z_, xl_, c_, xh_, y_):
        return (z_ * 4 + xl_ * 2 + c_, xh_ * 4 + y_)

    zn, zv = (z + 1) % NZ, (z + NZ - 1) % NZ
    mate = at(z, xl, 1 - c, xh, y)
    side = at(z, 1 - xl, c, xh, y)
    side_mate = at(z, 1 - xl, 1 - c, xh, y)
    z_next = at(zn, xl, c, xh, y)
    z_prev = at(zv, xl, c, xh, y)
    side_next = at(zn, 1 - xl, c, xh, y)
    side_prev = at(zv, 1 - xl, c, xh, y)
    later = at((z + 4) % NZ, xl, c, xh, y)
    earlier = at((z + NZ - 4) % NZ, xl, c, xh, y)
    six_up = at((z + 6) % NZ, xl, c, xh, y)
    six_down = at((z + NZ - 6) % NZ, xl, c, xh, y)

    def rc(src, dst, sems, i, dev):
        return pltpu.make_async_remote_copy(
            src_ref=src, dst_ref=dst, send_sem=sems.at[0, i], recv_sem=sems.at[1, i],
            device_id=dev, device_id_type=MESH)

    def rc2(src, dst, si, ri, sems, dev):
        return pltpu.make_async_remote_copy(
            src_ref=src, dst_ref=dst, send_sem=sems.at[0, si], recv_sem=sems.at[1, ri],
            device_id=dev, device_id_type=MESH)

    rows = pl.ds(pl.multiple_of(xl * 128, 128), 128)
    others = pl.ds(pl.multiple_of((1 - xl) * 128, 128), 128)
    r0 = pl.ds(pl.multiple_of(xl * 128 + c * 64, 64), 64)
    mine = pl.ds(pl.multiple_of(c * 128, 128), 128)
    theirs = pl.ds(pl.multiple_of((1 - c) * 128, 128), 128)

    own_w = pltpu.make_async_copy(w_in.at[:, :, mine], w.at[z, pl.ds(0, 3), r0, :], s_tok.at[0, 2])
    own_o = pltpu.make_async_copy(wo_in.at[:, mine], w.at[z, 3, r0, :], s_tok.at[0, 3])
    own_tok = pltpu.make_async_copy(tok_in, tok.at[c], s_tok.at[0, 1])
    for d in (own_w, own_o, own_tok):
        d.start()

    bar = pltpu.get_barrier_semaphore()

    def greet(dev):
        pl.semaphore_signal(bar, inc=1, device_id=dev, device_id_type=MESH)

    kv[...] = jnp.zeros_like(kv)
    for dev in (six_up, six_down, later, earlier, z_next, z_prev, side_next, side_prev, side_mate, mate):
        greet(dev)
    for dx in range(4):
        for dy in range(4):
            if dx or dy:
                greet(at(z, xl ^ (dx & 1), c, xh ^ (dx >> 1), (y + dy) % 4))
    for dx, dy in ((2, 0), (0, 1), (0, 2), (0, 3), (2, 1), (2, 2), (2, 3)):
        greet(at(z, xl, 1 - c, xh ^ (dx >> 1), (y + dy) % 4))
    pl.semaphore_wait(bar, 32)

    i_mate = rc(w_in.at[:, :, theirs], w.at[z, pl.ds(0, 3), r0, :], s_init, 0, mate)
    i_side = rc(w_in.at[0, :, mine], w.at[z, 0, r0, :], s_init, 1, side)
    i_diag = rc(w_in.at[0, :, theirs], w.at[z, 0, r0, :], s_init, 2, side_mate)
    i_out = rc(wo_in.at[:, theirs], w.at[z, 3, r0, :], s_init, 3, mate)
    i_mate.start()
    i_out.start()
    i_side.start()
    i_diag.start()
    tok_x = rc(tok_in, tok.at[c], s_tok, 0, mate)
    tok_x.start()

    def chunk(zo, ch):
        return w.at[zo, (1, 2, 0, 0, 3)[ch], others if ch == 3 else rows, :]

    def zp_copy(zo, ch, s):
        return rc(chunk(zo, ch), chunk(zo, ch), s_zp, ch * 8 + s, z_next)

    def zm_copy(zo, ch, s):
        return rc(chunk(zo, ch), chunk(zo, ch), s_zm, ch * 8 + s, z_prev)

    def x_copy(zo, m, i):
        return rc(chunk(zo, m), chunk(zo, m), s_x, m * 16 + i, side)

    own_w.wait()
    i_mate.wait_recv()
    for ch in range(2):
        zp_copy(z, ch, 0).start()
        zm_copy(z, ch, 0).start()
        x_copy(z, ch, 0).start()
    zp_copy(z, 2, 0).start()
    zm_copy(z, 2, 0).start()
    own_o.wait()
    i_out.wait_recv()
    i_side.wait_recv()
    i_diag.wait_recv()
    for ch in (3, 4):
        zp_copy(z, ch, 0).start()
        zm_copy(z, ch, 0).start()

    rh, rw, rt = win[c, 1], win[c, 2], win[c, 0]
    qi = lax.broadcasted_iota(jnp.int32, (64, 384), 0)
    ki = lax.broadcasted_iota(jnp.int32, (64, 384), 1)
    grp = ki // 128
    krow = (ki % 128) // 8
    d_r = jnp.abs(krow - 4 - qi // 8)
    d_c = jnp.abs((grp - 1) * 8 + ki % 8 - qi % 8)
    grow = h * 8 + krow - 4
    near = (d_r <= rh) & (d_c <= rw) & (grow >= 0) & (grow < 32)
    for u in range(4):
        gcol = xl * 4 + u + grp - 1
        mask[u] = jnp.where(near & (gcol >= 0) & (gcol < 8), F32(1.0), F32(0.0))

    def allow(a, f):
        df = 2 + a - f
        ok = jnp.where(rt >= df, F32(1.0), F32(0.0))
        if f < 2:
            ok = jnp.where(t > 0, ok, F32(0.0))
        return ok

    def project(zo):
        cols = pl.ds(pl.multiple_of(zo * 256, 256), 256)
        lhs = tok[:, :, cols].reshape(512, 256)
        rhs = jnp.concatenate([w[zo, 0], w[zo, 1], w[zo, 2]], axis=1)
        return jnp.dot(lhs, rhs, preferred_element_type=F32)

    def take(s, ch):
        zp, zm = (z + NZ - s) % NZ, (z + s) % NZ
        last_p, last_m = (8, 7) if ch in (2, 3) else (7, 8)

        @pl.when(s <= last_p)
        def _():
            zp_copy(zp, ch, s - 1).wait_recv()

            @pl.when(s < last_p)
            def _():
                zp_copy(zp, ch, s).start()
            if ch < 2:
                x_copy(zp, ch, s).start()

        @pl.when(s <= last_m)
        def _():
            zm_copy(zm, ch, s - 1).wait_recv()

            @pl.when(s < last_m)
            def _():
                zm_copy(zm, ch, s).start()
            if ch < 2:
                x_copy(zm, ch, 7 + s).start()

    def both_sides(s):
        zq = (z + NZ - s) % NZ
        x_copy(zq, 0, s).wait_recv()
        x_copy(zq, 1, s).wait_recv()
        acc[...] += project(zq)
        zr = (z + s) % NZ
        x_copy(zr, 0, 7 + s).wait_recv()
        x_copy(zr, 1, 7 + s).wait_recv()
        acc[...] += project(zr)

    def fwd(s, _):
        for ch in range(5):
            take(s, ch)

        @pl.when(s == 1)
        def _():
            own_tok.wait()
            tok_x.wait_recv()
            x_copy(z, 0, 0).wait_recv()
            x_copy(z, 1, 0).wait_recv()
            acc[...] = project(z)

        @pl.when(s > 1)
        def _():
            both_sides(s - 1)
        return 0

    lax.fori_loop(1, 8, fwd, 0)
    take(8, 0)
    take(8, 1)
    both_sides(7)
    z8 = (z + 8) % NZ
    x_copy(z8, 0, 15).wait_recv()
    x_copy(z8, 1, 15).wait_recv()
    lhs8 = tok[:, :, pl.ds(pl.multiple_of(z8 * 256, 256), 256)].reshape(512, 256)
    acc[:, 128:384] += jnp.dot(lhs8, jnp.concatenate([w[z8, 1], w[z8, 2]], axis=1), preferred_element_type=F32)

    def unit(p):
        return p * lax.rsqrt(jnp.mean(p * p, axis=-1, keepdims=True) + 1e-06)

    edge_out = 4 - 3 * xl
    edge_in = 5 * xl
    OWN, TOP, BOT = pl.ds(32, 64), pl.ds(0, 32), pl.ds(96, 32)
    UP, DOWN = pl.ds(32, 32), pl.ds(64, 32)
    MIDG = pl.ds(1, 4)
    FRAMES = (pl.ds(2, 2), pl.ds(1, 1), pl.ds(0, 1))

    def t_halo(f):
        grp = MIDG if f else pl.ds(1, 2)
        return rc(kv.at[2 + f, grp, OWN, :], kv.at[f, grp, OWN, :], s_t, f, later)

    far_1 = rc(kv.at[2, pl.ds(3, 2), OWN, :], relay, s_far, 0, six_down)
    far_2 = rc(relay, kv.at[0, pl.ds(3, 2), OWN, :], s_far, 1, six_down)
    has_relay = (z + 6) % NZ < 12

    def h_down(i):
        return rc(kv.at[FRAMES[i], MIDG, DOWN, :], kv.at[FRAMES[i], MIDG, TOP, :], s_h, i, z_next)

    def h_up(i):
        return rc(kv.at[FRAMES[i], MIDG, UP, :], kv.at[FRAMES[i], MIDG, BOT, :], s_h, 3 + i, z_prev)

    def x_own(i):
        return rc(kv.at[FRAMES[i], edge_out, OWN, :], kv.at[FRAMES[i], edge_in, OWN, :], s_xe, i, side)

    def x_down(i):
        return rc(kv.at[FRAMES[i], edge_out, DOWN, :], kv.at[FRAMES[i], edge_in, TOP, :], s_xe, 3 + i, side_next)

    def x_up(i):
        return rc(kv.at[FRAMES[i], edge_out, UP, :], kv.at[FRAMES[i], edge_in, BOT, :], s_xe, 6 + i, side_prev)

    has_prev, has_later = t > 0, t < 3
    has_up, has_down = h > 0, h < 3

    def halo_start(i):
        @pl.when(has_down)
        def _():
            h_down(i).start()
            x_down(i).start()

        @pl.when(has_up)
        def _():
            h_up(i).start()
            x_up(i).start()
        x_own(i).start()

    def halo_wait(i):
        x_own(i).wait_recv()

        @pl.when(has_up)
        def _():
            h_down(i).wait_recv()
            x_down(i).wait_recv()

        @pl.when(has_down)
        def _():
            h_up(i).wait_recv()
            x_up(i).wait_recv()

    def halo_sent(i):
        x_own(i).wait_send()

        @pl.when(has_down)
        def _():
            h_down(i).wait_send()
            x_down(i).wait_send()

        @pl.when(has_up)
        def _():
            h_up(i).wait_send()
            x_up(i).wait_send()

    def place(a):
        for tw in range(2):
            at_rows = pl.ds(tw * 256 + a * 128, 128)
            both = jnp.concatenate([unit(acc[at_rows, 128:256]), acc[at_rows, 256:384]], axis=1)
            both = both.reshape(8, 2, 8, 256)
            for g in range(2):
                kv[2 + a, 1 + tw * 2 + g, 32:96, :] = both[:, g].reshape(64, 256).astype(BF16)

    place(1)

    @pl.when(has_later)
    def _():
        t_halo(1).start()
    place(0)

    @pl.when(has_later)
    def _():
        far_1.start()
    halo_start(0)

    for ch in (2, 3, 4):
        take(8, ch)

    def wa(dx, dy):
        xh2, y2 = xh ^ (dx >> 1), (y + dy) % 4
        j2 = xh2 * 4 + y2
        src = w.at[pl.ds(2 * j2, 2), 3, rows, :]
        return rc(src, wo.at[c, xh * 4 + y, xl], s_wa, dx * 4 + dy, at(z, xl ^ (dx & 1), c, xh2, y2))

    for dx in range(4):
        for dy in range(4):
            if dx or dy:
                wa(dx, dy).start()
    own_wo = pltpu.make_async_copy(w.at[pl.ds(2 * te, 2), 3, rows, :], wo.at[c, te, xl], s_wa.at[0, 0])
    own_wo.start()

    acc[:, 0:128] += jnp.dot(
        tok[:, :, pl.ds(pl.multiple_of(z8 * 256, 256), 256)].reshape(512, 256), w[z8, 0], preferred_element_type=F32)
    for tw in range(2):
        for a in range(2):
            q = unit(acc[pl.ds(tw * 256 + a * 128, 128), 0:128]).reshape(8, 2, 8, 128)
            for g in range(2):
                qs[tw * 2 + g, a] = q[:, g].reshape(64, 128).astype(BF16)

    def attend(u, a, f):
        keys = kv[f, u:u + 3, :, 0:128].reshape(384, 128)
        vals = kv[f, u:u + 3, :, 128:256].reshape(384, 128)
        s = lax.dot_general(qs[u, a], keys, (((1,), (1,)), ((), ())), preferred_element_type=F32)
        wt = jnp.exp(s * SCALE) * (mask[u] * allow(a, f))
        part = wt[:, 0:128] + wt[:, 128:256] + wt[:, 256:384]
        return jnp.dot(wt.astype(BF16), vals, preferred_element_type=F32), part

    halo_wait(0)
    for u in range(4):
        o, p = attend(u, 0, 2)
        os[u, 0] = o
        ts[u, 0] = p
        o2, p2 = attend(u, 1, 2)
        o3, p3 = attend(u, 1, 3)
        os[u, 1] = o2 + o3
        ts[u, 1] = p2 + p3

    @pl.when(has_later)
    def _():
        t_halo(0).start()

    te_x = (1 - xh) * 4 + y

    def slot(a, k, dy, p):
        return ((a * 2 + k) * 4 + dy) * 2 + p

    def a_out(a, k, dy, own):
        src = att.at[te, c, a] if own else tmp.at[1 - c, a]
        dev = at(z, xl, c if own else 1 - c, 1 - xh if k else xh, (y + dy) % 4)
        return rc2(src, att.at[te, c, a], slot(a, k, dy, 0 if own else 1), slot(a, k, dy, c), s_ag, dev)

    def a_in(a, k, dy, p):
        return rc(att.at[te, p, a], att.at[te, p, a], s_ag, slot(a, k, dy, p), mate)

    def finish(a, f):
        for u in range(4):
            o, p = attend(u, a, f)
            total = jnp.sum(ts[u, a] + p, axis=-1, keepdims=True)
            res = (os[u, a] + o) / total
            attf[u // 2, :, u % 2] = res.reshape(8, 8, 128)
        for tw in range(2):
            tmp[tw, a] = attf[tw].reshape(128, 128).astype(BF16)
        att[te, c, a] = tmp[c, a]
        for k, dy in ROUTE:
            if k or dy:
                a_out(a, k, dy, True).start()
            a_out(a, k, dy, False).start()

    def term(j, a):
        lhs = jnp.concatenate([att[j, 0, a], att[j, 1, a]], axis=1)
        rhs = jnp.concatenate([
            jnp.concatenate([wo[0, j, x, k], wo[1, j, x, k]], axis=1)
            for k in range(2) for x in range(2)], axis=0)
        return lax.dot_general(lhs, rhs, (((1,), (1,)), ((), ())), preferred_element_type=F32)

    def mix(a):
        tot = fin.at[a]
        for k, dy in ROUTE[::-1]:
            if k or dy:
                a_in(a, k, dy, 0).wait_recv()
                a_in(a, k, dy, 1).wait_recv()
                xs = 1 - xh if k else xh
                tot[...] += term(xs * 4 + (y + 4 - dy) % 4, a)
            else:
                rc2(att.at[te, 0, a], att.at[te, 0, a], 0, slot(a, 0, 0, 1 - c), s_ag, mate).wait_recv()
                tot[...] = term(te, a)
        out[a * 128:(a + 1) * 128, :] = tot[...].astype(BF16)

    @pl.when(has_prev)
    def _():
        t_halo(1).wait_recv()
        halo_start(1)

    @pl.when(has_relay)
    def _():
        far_1.wait_recv()
        far_2.start()

    @pl.when(has_prev)
    def _():
        halo_wait(1)
    finish(1, 1)

    for u in range(4):
        o, p = attend(u, 0, 1)
        os[u, 0] += o
        ts[u, 0] += p
    own_wo.wait()
    for dx in range(4):
        for dy in range(4):
            if dx or dy:
                wa(dx, dy).wait_recv()
    wo_x = rc(wo.at[c], wo.at[c], s_wc, 0, mate)
    wo_x.start()

    @pl.when(has_prev)
    def _():
        t_halo(0).wait_recv()
        far_2.wait_recv()
        halo_start(2)

    @pl.when(has_prev)
    def _():
        halo_wait(2)
    finish(0, 0)
    wo_x.wait_recv()
    mix(1)
    mix(0)

    for d in (i_mate, i_side, i_diag, i_out, tok_x, wo_x):
        d.wait_send()

    def drain(s, _):
        for m in range(2):
            x_copy(z, m, s).wait_send()

        @pl.when(s < 8)
        def _():
            for ch in range(5):
                (zp_copy if ch in (2, 3) else zm_copy)(z, ch, s).wait_send()

        @pl.when(s < 7)
        def _():
            for ch in range(5):
                (zm_copy if ch in (2, 3) else zp_copy)(z, ch, s).wait_send()
        return 0

    lax.fori_loop(0, 16, drain, 0)
    for dx in range(4):
        for dy in range(4):
            if dx or dy:
                wa(dx, dy).wait_send()
    for a in range(2):
        for k, dy in ROUTE:
            if k or dy:
                a_out(a, k, dy, True).wait_send()
            a_out(a, k, dy, False).wait_send()
    halo_sent(0)

    @pl.when(has_later)
    def _():
        t_halo(0).wait_send()
        t_halo(1).wait_send()
        far_1.wait_send()

    @pl.when(has_relay)
    def _():
        far_2.wait_send()

    @pl.when(has_prev)
    def _():
        halo_sent(1)
        halo_sent(2)


def per_device(tokens, w_qkv, w_out, window_ext):
    vm = pl.BlockSpec(memory_space=pltpu.VMEM)
    hbm = pl.BlockSpec(memory_space=pl.ANY)
    dma = lambda n: pltpu.SemaphoreType.DMA((2, n))
    return pl.pallas_call(
        kernel,
        out_shape=jax.ShapeDtypeStruct((256, 512), BF16),
        in_specs=[pl.BlockSpec(memory_space=pltpu.SMEM), hbm, hbm, hbm],
        out_specs=vm,
        scratch_shapes=[
            pltpu.VMEM((2, 256, 4096), BF16),
            pltpu.VMEM((16, 4, 256, 128), BF16),
            pltpu.VMEM((512, 384), F32),
            pltpu.VMEM((4, 6, 128, 256), BF16),
            pltpu.VMEM((4, 2, 64, 128), BF16),
            pltpu.VMEM((4, 64, 384), F32),
            pltpu.VMEM((4, 2, 64, 128), F32),
            pltpu.VMEM((4, 2, 64, 128), F32),
            pltpu.VMEM((2, 8, 2, 8, 128), F32),
            pltpu.VMEM((8, 2, 2, 128, 128), BF16),
            pltpu.VMEM((2, 2, 128, 128), BF16),
            pltpu.VMEM((2, 8, 2, 2, 128, 128), BF16),
            pltpu.VMEM((2, 128, 512), F32),
            pltpu.VMEM((2, 64, 256), BF16),
            dma(4), dma(4), dma(40), dma(40), dma(32), dma(2), dma(6), dma(9),
            dma(16), dma(1), dma(32), dma(2),
        ],
        compiler_params=pltpu.CompilerParams(
            collective_id=0, has_side_effects=True, vmem_limit_bytes=56 * 2 ** 20),
        name="tile_attention",
    )(window_ext, tokens, w_qkv, w_out.T)


def solution(mesh):
    in_specs = (P("tile", None), P(None, "tile", "tensor"), P("tensor", "tile"), P("tensor", None))
    return jax.shard_map(
        per_device, mesh=mesh, in_specs=in_specs, out_specs=P("tile", "tensor"), check_vma=False)
```
